32 devices in a mesh: depth: 8 (over z, x), rows: 4 (over y, core).
Axes of the slice: x: 2, y: 2, z: 4, core: 2. Of those that a mesh axis runs over, the one named last changes fastest.
Arguments:
- spectrum: bfloat16 [2, 4096, 4096], P(None, 'rows'), may hold values from -6 to 6
- plane_index: int32 [8], P('depth'), may hold values from 0 to 2047
- kernel_width: int32 [8], P('depth'), may hold values from 1 to 3
- focus_gain: float32 [8], P('depth'), may hold values from 0.5 to 30
Outputs:
- depth_map: float32 [256, 4096], P('rows', 'depth')
- focused: float32 [2, 256, 4096], P(None, 'rows', 'depth')
The draws below stay inside these ranges and needn't reach their ends.
All inputs are finite; a program needn't handle non-finite values.
Results may differ from the reference program's by a relative error of at most 0.0003.
Values may be sent and summed in bfloat16 or wider, within the bound.
A program may use at most 192 MiB of HBM per device.

```python
import math
import jax
import jax.numpy as jnp
from jax import lax

NX = 4096
Y_WIN = 256
DEPTHS = 2048
MAXWIDTH = 3
N_PLANES = 8


def draw_focus_gain(key, part):
    values = jnp.exp(jax.random.uniform(key, (N_PLANES,), jnp.float32, jnp.log(0.5), jnp.log(4.0)))
    return values


def place_ends(result, stream_key, smallest, top_value):
    shape = result.shape
    spot = [jax.random.randint(jax.random.fold_in(stream_key, axis), (), 0, shape[axis]) for axis in range(len(shape))]
    result = result.at[tuple(spot)].set(smallest)
    longest = shape.index(max(shape))
    spot[longest] = (spot[longest] + 1) % shape[longest]
    return result.at[tuple(spot)].set(top_value)


def shard_levels(stream_key, shape, pieces, least, top_value):
    def one(dim, shards_of):
        heights = jax.random.uniform(jax.random.fold_in(jax.random.fold_in(stream_key, 6), dim), (shards_of,), jnp.float32, least / len(pieces), top_value / len(pieces))
        return jnp.repeat(jnp.exp(heights), shape[dim] // shards_of).reshape((-1,) + (1,) * (len(shape) - dim - 1))

    factor_of = one(*pieces[0])
    for cut in pieces[1:]:
        factor_of = factor_of * one(*cut)
    return factor_of


def centred(rng, dims, spread, bound, split=(), kind=jnp.bfloat16):
    level = shard_levels(rng, dims, split, -0.22, 0.18) if split else 1.0
    result = jax.random.normal(rng, dims, jnp.float32) * spread * level
    return jnp.minimum(jnp.maximum(result, -bound), bound).astype(kind)


def setup_inputs(seed: int = 0) -> dict:
    keys = jax.random.split(jax.random.key(seed), 5)
    return {
        "spectrum": centred(keys[0], (2, NX, NX), 1.0, 6.0, ((1, 4),)),
        "plane_index": place_ends(jax.random.randint(keys[1], (N_PLANES,), 0, DEPTHS), jax.random.fold_in(keys[1], 1), 0, DEPTHS - 1).astype(jnp.int32),
        "kernel_width": place_ends(jax.random.randint(keys[2], (N_PLANES,), 1, MAXWIDTH + 1), jax.random.fold_in(keys[2], 1), 1, MAXWIDTH).astype(jnp.int32),
        "focus_gain": draw_focus_gain(jax.random.fold_in(keys[4], 71), 0),
    }


def line_phase(plane_index, freqs):
    signed = jnp.where(freqs < NX // 2, freqs, freqs - NX)
    square = signed * signed
    upper_part = (square // NX)[None, :]
    lower_part = (square % NX)[None, :]
    depth_col = plane_index[:, None]
    turns = (depth_col * lower_part + NX * ((depth_col * upper_part) % NX)) % (NX * NX)
    return turns.astype(jnp.float32) * (-2.0 * math.pi / (NX * NX))


def sobel_energy(padded):
    vertical = padded[..., :-2, :] + 2.0 * padded[..., 1:-1, :] + padded[..., 2:, :]
    across = vertical[..., :, 2:] - vertical[..., :, :-2]
    horizontal = padded[..., :, :-2] + 2.0 * padded[..., :, 1:-1] + padded[..., :, 2:]
    downward = horizontal[..., 2:, :] - horizontal[..., :-2, :]
    return across * across + downward * downward


def smooth_columns(energy, radius):
    extent = energy.shape[-1]
    padded = jnp.pad(energy, [(0, 0)] * (energy.ndim - 1) + [(MAXWIDTH, MAXWIDTH)])
    summed = jnp.zeros_like(energy)
    for offset in range(-MAXWIDTH, MAXWIDTH + 1):
        inside = (abs(offset) <= radius).astype(jnp.float32)
        summed = summed + inside * padded[..., MAXWIDTH + offset:MAXWIDTH + offset + extent]
    return summed / (2 * radius + 1).astype(jnp.float32)


def reference(spectrum, plane_index, kernel_width, focus_gain):
    spectra = spectrum.astype(jnp.float32)
    freqs = jnp.arange(NX, dtype=jnp.int32)

    def advance(records, inputs):
        depth_number, radius, sharpness = inputs
        phases = line_phase(depth_number[None], freqs)[0]
        cosine = jnp.cos(phases)
        sine_part = jnp.sin(phases)
        factor_real = cosine[:, None] * cosine[None, :] - sine_part[:, None] * sine_part[None, :]
        factor_imag = cosine[:, None] * sine_part[None, :] + sine_part[:, None] * cosine[None, :]
        rot_real = spectra[0] * factor_real - spectra[1] * factor_imag
        rot_imag = spectra[0] * factor_imag + spectra[1] * factor_real
        picture = jnp.fft.ifft2(lax.complex(rot_real, rot_imag))[:Y_WIN] * NX
        real_part = jnp.real(picture)
        imag_part = jnp.imag(picture)
        intensity = real_part * real_part + imag_part * imag_part
        energy = sobel_energy(jnp.pad(intensity, 1))
        scores = sharpness * jnp.log(1.0 + smooth_columns(energy, radius))
        highest, summed, depth_sum, real_sum, imag_sum = records
        peak = jnp.maximum(highest, scores)
        former = jnp.exp(highest - peak)
        latest = jnp.exp(scores - peak)
        depth_value = depth_number.astype(jnp.float32) / DEPTHS
        updated = (peak, summed * former + latest, depth_sum * former + latest * depth_value,
                   real_sum * former + latest * real_part, imag_sum * former + latest * imag_part)
        return updated, None

    starting = jnp.full((Y_WIN, NX), -1e30, jnp.float32)
    zeros_grid = jnp.zeros((Y_WIN, NX), jnp.float32)
    records, unused = lax.scan(advance, (starting, zeros_grid, zeros_grid, zeros_grid, zeros_grid),
                               (plane_index, kernel_width, focus_gain))
    highest, summed, depth_sum, real_sum, imag_sum = records
    depth_map = depth_sum / summed
    focused = jnp.stack([real_sum / summed, imag_sum / summed])
    return depth_map, focused
```

```python
from functools import partial
import math

import numpy as np
import jax
import jax.numpy as jnp
from jax import lax
from jax.experimental import pallas as pl
from jax.experimental.pallas import tpu as pltpu
from jax.sharding import PartitionSpec as P

NX = 4096
Y_WIN = 256
DEPTHS = 2048
MAXWIDTH = 3
LANES = 128
SLABS = NX // LANES
CORES = 2
LAG = 3
VMEM_BYTES = 56 * 1024 * 1024


def line_phase(plane, freqs):
    signed = jnp.where(freqs < NX // 2, freqs, freqs - NX)
    square = signed * signed
    turns = (plane * (square % NX) + NX * (plane * (square // NX) % NX)) % (NX * NX)
    return turns.astype(jnp.float32) * (-2.0 * math.pi / (NX * NX))


def row_table(plane, place, count):
    freqs_n = NX // count
    band = Y_WIN // count
    turns = np.arange(Y_WIN)[:, None] * np.arange(freqs_n)[None, :] % NX
    angle = turns * (2.0 * np.pi / NX)
    base_cos = jnp.asarray(np.cos(angle).astype(np.float32))
    base_sin = jnp.asarray(np.sin(angle).astype(np.float32))
    phase = line_phase(plane, place * freqs_n + jnp.arange(freqs_n, dtype=jnp.int32))
    start = place * freqs_n * jnp.arange(Y_WIN, dtype=jnp.int32) % NX
    start_angle = start.astype(jnp.float32) * (2.0 * math.pi / NX)
    col_cos, col_sin = jnp.cos(phase)[None, :], jnp.sin(phase)[None, :]
    row_cos, row_sin = jnp.cos(start_angle)[:, None], jnp.sin(start_angle)[:, None]
    turn_cos = row_cos * col_cos - row_sin * col_sin
    turn_sin = row_cos * col_sin + row_sin * col_cos
    real = base_cos * turn_cos - base_sin * turn_sin
    imag = base_cos * turn_sin + base_sin * turn_cos
    upper = jnp.concatenate([real, -imag], axis=1)
    lower = jnp.concatenate([imag, real], axis=1)
    table = jnp.stack([upper, lower]).reshape(2, count // CORES, CORES, band, 2 * freqs_n)
    table = table.transpose(2, 1, 0, 3, 4).reshape(2 * Y_WIN, 2 * freqs_n)
    first = lax.reduce_precision(table, 8, 7)
    return first.astype(jnp.bfloat16), (table - first).astype(jnp.bfloat16)


def row_kernel(count, chunks, first_ref, second_ref, spec_ref, out_ref,
               part, core_in, half, chip_in, a_send, a_recv, b_send, b_recv):
    chips = count // CORES
    step = pl.program_id(0)
    me = lax.axis_index("rows")
    core, chip = lax.rem(me, CORES), lax.div(me, CORES)
    half_rows = part.shape[1] // CORES
    block = half_rows // chips
    width = spec_ref.shape[1]
    partner = chip * CORES + 1 - core

    def other(hop):
        return lax.rem(chip + hop, chips)

    def core_copy(k):
        rows = pl.ds(pl.multiple_of((1 - core) * half_rows, half_rows), half_rows)
        return pltpu.make_async_remote_copy(
            src_ref=part.at[k, rows], dst_ref=core_in.at[k],
            send_sem=a_send.at[k], recv_sem=a_recv.at[k],
            device_id={"rows": partner}, device_id_type=pl.DeviceIdType.MESH)

    def chip_copy(k, hop):
        rows = pl.ds(pl.multiple_of(other(hop) * block, block), block)
        return pltpu.make_async_remote_copy(
            src_ref=half.at[k, rows], dst_ref=chip_in.at[k, hop - 1],
            send_sem=b_send.at[k, hop - 1], recv_sem=b_recv.at[k, hop - 1],
            device_id={"rows": other(hop) * CORES + core}, device_id_type=pl.DeviceIdType.MESH)

    @pl.when(step == 0)
    def _():
        barrier = pltpu.get_barrier_semaphore()
        pl.semaphore_signal(barrier, inc=1, device_id={"rows": partner},
                            device_id_type=pl.DeviceIdType.MESH)
        for hop in range(1, chips):
            pl.semaphore_signal(barrier, inc=1, device_id={"rows": other(hop) * CORES + core},
                                device_id_type=pl.DeviceIdType.MESH)
        pl.semaphore_wait(barrier, chips)

    @pl.when(step < chunks)
    def _():
        part[step] = (
            jnp.dot(first_ref[...], spec_ref[...], preferred_element_type=jnp.float32)
            + jnp.dot(second_ref[...], spec_ref[...], preferred_element_type=jnp.float32))
        core_copy(step).start()

    @pl.when(jnp.logical_and(step >= 1, step < chunks + 1))
    def _():
        k = step - 1
        core_copy(k).wait()
        rows = pl.ds(pl.multiple_of(core * half_rows, half_rows), half_rows)
        half[k] = part[k, rows] + core_in[k]
        for hop in range(1, chips):
            chip_copy(k, hop).start()

    @pl.when(step >= LAG)
    def _():
        k = step - LAG
        rows = pl.ds(pl.multiple_of(chip * block, block), block)
        for hop in range(1, chips):
            chip_copy(k, hop).wait()
        total = half[k, rows]
        for hop in range(1, chips):
            total = total + chip_in[k, hop - 1]
        out_ref[:, pl.ds(pl.multiple_of(k * width, width), width)] = total


def row_transform(spectra, first, second, count):
    depth = spectra.shape[0]
    width = 512
    chunks = NX // width
    chips = count // CORES
    half_rows = 2 * Y_WIN // CORES
    block = half_rows // chips
    whole = pl.BlockSpec((2 * Y_WIN, depth), lambda c: (0, 0))
    return pl.pallas_call(
        partial(row_kernel, count, chunks),
        out_shape=jax.ShapeDtypeStruct((block, NX), jnp.float32),
        grid=(chunks + LAG,),
        in_specs=[whole, whole,
                  pl.BlockSpec((depth, width), lambda c: (0, jnp.minimum(c, chunks - 1)))],
        out_specs=pl.BlockSpec((block, NX), lambda c: (0, 0)),
        scratch_shapes=[
            pltpu.VMEM((chunks, 2 * Y_WIN, width), jnp.float32),
            pltpu.VMEM((chunks, half_rows, width), jnp.float32),
            pltpu.VMEM((chunks, half_rows, width), jnp.float32),
            pltpu.VMEM((chunks, chips - 1, block, width), jnp.float32),
            pltpu.SemaphoreType.DMA((chunks,)),
            pltpu.SemaphoreType.DMA((chunks,)),
            pltpu.SemaphoreType.DMA((chunks, chips - 1)),
            pltpu.SemaphoreType.DMA((chunks, chips - 1)),
        ],
        compiler_params=pltpu.CompilerParams(
            collective_id=0, has_side_effects=True, vmem_limit_bytes=VMEM_BYTES),
    )(first, second, spectra)


def butterflies(real, imag):
    n = len(real)
    if n == 1:
        return real, imag
    even_r, even_i = butterflies(real[0::2], imag[0::2])
    odd_r, odd_i = butterflies(real[1::2], imag[1::2])
    out_r, out_i = [None] * n, [None] * n
    for k in range(n // 2):
        c, s = math.cos(2.0 * math.pi * k / n), math.sin(2.0 * math.pi * k / n)
        if k == 0:
            tr, ti = odd_r[k], odd_i[k]
        elif 4 * k == n:
            tr, ti = -odd_i[k], odd_r[k]
        else:
            tr, ti = odd_r[k] * c - odd_i[k] * s, odd_r[k] * s + odd_i[k] * c
        out_r[k], out_i[k] = even_r[k] + tr, even_i[k] + ti
        out_r[k + n // 2], out_i[k + n // 2] = even_r[k] - tr, even_i[k] - ti
    return out_r, out_i


def column_kernel(strip_ref, phase_ref, twist_ref, table_ref, pic_ref, power_ref, mid):
    band = strip_ref.shape[0] // 2

    @pl.loop(0, band // 8)
    def _(s):
        at = pl.multiple_of(s * 8, 8)
        real, imag = [], []
        for slab in range(SLABS):
            lanes = slice(slab * LANES, (slab + 1) * LANES)
            xr = strip_ref[pl.ds(at, 8), lanes]
            xi = strip_ref[pl.ds(band + at, 8), lanes]
            pc, ps = phase_ref[0:1, lanes], phase_ref[1:2, lanes]
            real.append(xr * pc - xi * ps)
            imag.append(xr * ps + xi * pc)
        real, imag = butterflies(real, imag)
        for slab in range(SLABS):
            tc, ts = twist_ref[0, slab:slab + 1, :], twist_ref[1, slab:slab + 1, :]
            mid[slab, pl.ds(at, 8), 0:LANES] = real[slab] * tc - imag[slab] * ts
            mid[slab, pl.ds(at, 8), LANES:2 * LANES] = real[slab] * ts + imag[slab] * tc

    per = 4

    @pl.loop(0, SLABS // per)
    def _(q):
        slabs = pl.ds(q * per, per)
        rows = mid[slabs].reshape(per * band, 2 * LANES)
        both = jnp.dot(rows, table_ref[...], precision=lax.Precision.HIGHEST,
                       preferred_element_type=jnp.float32)
        real, imag = both[:, :LANES], both[:, LANES:]
        pic_ref[0, slabs] = real.reshape(per, band, LANES)
        pic_ref[1, slabs] = imag.reshape(per, band, LANES)
        power_ref[slabs] = (real * real + imag * imag).reshape(per, band, LANES)


def column_transform(strip, phase):
    band = strip.shape[0] // 2
    lane = np.arange(LANES)
    twist = np.arange(SLABS)[:, None] * lane[None, :] * (2.0 * np.pi / NX)
    twist = np.stack([np.cos(twist), np.sin(twist)]).astype(np.float32)
    angle = lane[:, None] * lane[None, :] % LANES * (2.0 * np.pi / LANES)
    cosine, sine = np.cos(angle) / NX, np.sin(angle) / NX
    table = np.block([[cosine, sine], [-sine, cosine]]).astype(np.float32)
    return pl.pallas_call(
        column_kernel,
        out_shape=(jax.ShapeDtypeStruct((2, SLABS, band, LANES), jnp.float32),
                   jax.ShapeDtypeStruct((SLABS, band, LANES), jnp.float32)),
        scratch_shapes=[pltpu.VMEM((SLABS, band, 2 * LANES), jnp.float32)],
        compiler_params=pltpu.CompilerParams(vmem_limit_bytes=VMEM_BYTES),
    )(strip, phase, jnp.asarray(twist), jnp.asarray(table))


def wrapped(block, forward):
    lane = lax.broadcasted_iota(jnp.int32, block.shape, block.ndim - 1)
    shift = LANES - 1 if forward else 1
    edge = LANES - 1 if forward else 0
    return jnp.where(lane == edge, 0.0, pltpu.roll(block, shift, block.ndim - 1))


def score_kernel(groups, smooth_ref, power_ref, low_ref, high_ref, pic_ref, out_ref,
                 rim, energy, score):
    band = power_ref.shape[1]
    rim[1:SLABS + 1, 8:8 + band, :] = power_ref[...]
    rim[1:SLABS + 1, 7:8, :] = low_ref[...]
    rim[1:SLABS + 1, 8 + band:9 + band, :] = high_ref[...]
    rim[0, 7:9 + band, :] = wrapped(rim[SLABS, 7:9 + band, :], False)
    rim[SLABS + 1, 7:9 + band, :] = wrapped(rim[1, 7:9 + band, :], True)

    @pl.loop(0, SLABS)
    def _(slab):
        def vertical(j):
            return rim[j, 7:7 + band, :] + 2.0 * rim[j, 8:8 + band, :] + rim[j, 9:9 + band, :]

        def horizontal(top):
            rows = slice(top, top + band)
            return rim[slab, rows, :] + 2.0 * rim[slab + 1, rows, :] + rim[slab + 2, rows, :]

        across = vertical(slab + 2) - vertical(slab)
        downward = horizontal(9) - horizontal(7)
        energy[slab + MAXWIDTH] = across * across + downward * downward

    for k in range(MAXWIDTH):
        energy[k] = wrapped(energy[SLABS + k], False)
        energy[SLABS + MAXWIDTH + k] = wrapped(energy[MAXWIDTH + k], True)

    @pl.loop(0, SLABS)
    def _(slab):
        total = energy[slab + MAXWIDTH]
        for k in range(1, MAXWIDTH + 1):
            total = total + smooth_ref[0, k] * (
                energy[slab + MAXWIDTH - k] + energy[slab + MAXWIDTH + k])
        score[slab] = smooth_ref[0, 4] * jnp.log(1.0 + total / smooth_ref[0, 0])

    per = SLABS // groups
    piece = LANES // per

    @pl.loop(0, band // 8)
    def _(s):
        at = pl.multiple_of(s * 8, 8)
        block_of = lax.broadcasted_iota(jnp.int32, (8, LANES), 1) // piece
        for kind in range(3):
            for g in range(groups):
                held = []
                for i in range(per):
                    slab = g * per + i
                    if kind == 0:
                        held.append(score[slab, pl.ds(at, 8), :])
                    else:
                        held.append(pic_ref[kind - 1, slab, pl.ds(at, 8), :])
                gap = 1
                while gap < per:
                    low_lane = block_of // gap % 2 == 0
                    for i in range(per):
                        if i // gap % 2 == 0:
                            a, c = held[i], held[i + gap]
                            held[i] = jnp.where(low_lane, a, pltpu.roll(c, gap * piece, 1))
                            held[i + gap] = jnp.where(
                                low_lane, pltpu.roll(a, LANES - gap * piece, 1), c)
                    gap *= 2
                for d in range(per):
                    out_ref[d, pl.ds(kind * band + at, 8), g * LANES:(g + 1) * LANES] = held[d]

    for d in range(per):
        out_ref[d, 3 * band:3 * band + 8, :] = jnp.full((8, groups * LANES), smooth_ref[0, 5])


def score_records(smooth, power, low, high, pic, targets):
    band = power.shape[1]
    groups = SLABS // targets
    vmem = pl.BlockSpec(memory_space=pltpu.VMEM)
    return pl.pallas_call(
        partial(score_kernel, groups),
        out_shape=jax.ShapeDtypeStruct((targets, 3 * band + 8, groups * LANES), jnp.float32),
        in_specs=[pl.BlockSpec(memory_space=pltpu.SMEM), vmem, vmem, vmem, vmem],
        out_specs=vmem,
        scratch_shapes=[
            pltpu.VMEM((SLABS + 2, band + 16, LANES), jnp.float32),
            pltpu.VMEM((SLABS + 2 * MAXWIDTH, band, LANES), jnp.float32),
            pltpu.VMEM((SLABS, band, LANES), jnp.float32),
        ],
        compiler_params=pltpu.CompilerParams(vmem_limit_bytes=VMEM_BYTES),
    )(smooth, power, low, high, pic)


def merge_kernel(rec_ref, order_ref, map_ref, field_ref):
    planes, rows_all, _ = rec_ref.shape
    band = (rows_all - 8) // 3
    peak = rec_ref[0, 0:band, :]
    for p in range(1, planes):
        peak = jnp.maximum(peak, rec_ref[p, 0:band, :])
    summed = jnp.zeros_like(peak)
    totals = [jnp.zeros_like(peak) for _ in range(3)]
    for p in range(planes):
        weight = jnp.exp(rec_ref[p, 0:band, :] - peak)
        summed = summed + weight
        totals[0] = totals[0] + weight * rec_ref[p, 3 * band:3 * band + 1, :]
        totals[1] = totals[1] + weight * rec_ref[p, band:2 * band, :]
        totals[2] = totals[2] + weight * rec_ref[p, 2 * band:3 * band, :]
    merged = jnp.concatenate([total / summed for total in totals], axis=0)
    placed = jnp.zeros_like(merged)
    for _ in range(3):
        term = merged.astype(jnp.bfloat16)
        placed = placed + jnp.dot(term, order_ref[...], preferred_element_type=jnp.float32)
        merged = merged - term.astype(jnp.float32)
    map_ref[...] = placed[0:band]
    field_ref[0] = placed[band:2 * band]
    field_ref[1] = placed[2 * band:3 * band]


def merge(records):
    planes, rows_all, width = records.shape
    band = (rows_all - 8) // 3
    per = SLABS // (width // LANES)
    piece = LANES // per
    spot = np.arange(width)
    slab = spot // LANES * per + spot % LANES // piece
    order = np.zeros((width, width), np.float32)
    order[spot, spot % piece * SLABS + slab] = 1.0
    return pl.pallas_call(
        merge_kernel,
        out_shape=(jax.ShapeDtypeStruct((band, width), jnp.float32),
                   jax.ShapeDtypeStruct((2, band, width), jnp.float32)),
        compiler_params=pltpu.CompilerParams(vmem_limit_bytes=VMEM_BYTES),
    )(records, jnp.asarray(order, jnp.bfloat16))


def shards(spectrum, plane_index, kernel_width, focus_gain):
    count = lax.axis_size("rows")
    targets = lax.axis_size("depth")
    place = lax.axis_index("rows")
    plane, radius = plane_index[0], kernel_width[0]
    first, second = row_table(plane, place, count)
    spectra = spectrum.reshape(2 * spectrum.shape[1], NX)
    strip = row_transform(spectra, first, second, count)
    phase = line_phase(plane, jnp.arange(NX, dtype=jnp.int32))
    pic, power = column_transform(strip, jnp.stack([jnp.cos(phase), jnp.sin(phase)]))
    band = power.shape[1]
    forward = [(i, i + 1) for i in range(count - 1)]
    backward = [(i + 1, i) for i in range(count - 1)]
    low = lax.ppermute(power[:, band - 1:, :], "rows", forward)
    high = lax.ppermute(power[:, :1, :], "rows", backward)
    inside = (jnp.arange(1, MAXWIDTH + 1) <= radius).astype(jnp.float32)
    smooth = jnp.concatenate([
        (2 * radius + 1).astype(jnp.float32)[None], inside, focus_gain,
        plane_index.astype(jnp.float32) / DEPTHS])[None]
    records = score_records(smooth, power, low, high, pic, targets)
    records = lax.all_to_all(records, "depth", split_axis=0, concat_axis=0, tiled=True)
    return merge(records)


def solution(mesh):
    return jax.shard_map(
        shards,
        mesh=mesh,
        in_specs=(P(None, "rows", None), P("depth"), P("depth"), P("depth")),
        out_specs=(P("rows", "depth"), P(None, "rows", "depth")),
        check_vma=False,
    )
```

```python
from functools import partial
import math

import numpy as np
import jax
import jax.numpy as jnp
from jax import lax
from jax.experimental import pallas as pl
from jax.experimental.pallas import tpu as pltpu
from jax.sharding import PartitionSpec as P

NX = 4096
Y_WIN = 256
DEPTHS = 2048
MAXWIDTH = 3
LANES = 128
SLABS = NX // LANES
CORES = 2
LAG = 3
STRIP = 16
STEPS = 32767.0
TINY = 1e-33
VMEM_BYTES = 56 * 1024 * 1024


def line_phase(plane, freqs):
    signed = jnp.where(freqs < NX // 2, freqs, freqs - NX)
    square = signed * signed
    turns = (plane * (square % NX) + NX * (plane * (square // NX) % NX)) % (NX * NX)
    return turns.astype(jnp.float32) * (-2.0 * math.pi / (NX * NX))


def row_table(plane, place, count):
    freqs_n = NX // count
    band = Y_WIN // count
    turns = np.arange(Y_WIN)[:, None] * np.arange(freqs_n)[None, :] % NX
    angle = turns * (2.0 * np.pi / NX)
    base_cos = jnp.asarray(np.cos(angle).astype(np.float32))
    base_sin = jnp.asarray(np.sin(angle).astype(np.float32))
    phase = line_phase(plane, place * freqs_n + jnp.arange(freqs_n, dtype=jnp.int32))
    start = place * freqs_n * jnp.arange(Y_WIN, dtype=jnp.int32) % NX
    start_angle = start.astype(jnp.float32) * (2.0 * math.pi / NX)
    col_cos, col_sin = jnp.cos(phase)[None, :], jnp.sin(phase)[None, :]
    row_cos, row_sin = jnp.cos(start_angle)[:, None], jnp.sin(start_angle)[:, None]
    turn_cos = row_cos * col_cos - row_sin * col_sin
    turn_sin = row_cos * col_sin + row_sin * col_cos
    real = base_cos * turn_cos - base_sin * turn_sin
    imag = base_cos * turn_sin + base_sin * turn_cos
    upper = jnp.concatenate([real, -imag], axis=1)
    lower = jnp.concatenate([imag, real], axis=1)
    table = jnp.stack([upper, lower]).reshape(2, count // CORES, CORES, band, 2 * freqs_n)
    table = table.transpose(2, 1, 0, 3, 4).reshape(2 * Y_WIN, 2 * freqs_n)
    first = lax.reduce_precision(table, 8, 7)
    return first.astype(jnp.bfloat16), (table - first).astype(jnp.bfloat16)


def row_kernel(count, chunks, first_ref, second_ref, spec_ref, out_ref,
               part, core_in, half, chip_in, a_send, a_recv, b_send, b_recv):
    chips = count // CORES
    step = pl.program_id(0)
    me = lax.axis_index("rows")
    core, chip = lax.rem(me, CORES), lax.div(me, CORES)
    half_rows = part.shape[1] // CORES
    block = half_rows // chips
    width = spec_ref.shape[1]
    partner = chip * CORES + 1 - core

    def other(hop):
        return lax.rem(chip + hop, chips)

    def core_copy(k):
        rows = pl.ds(pl.multiple_of((1 - core) * half_rows, half_rows), half_rows)
        return pltpu.make_async_remote_copy(
            src_ref=part.at[k, rows], dst_ref=core_in.at[k],
            send_sem=a_send.at[k], recv_sem=a_recv.at[k],
            device_id={"rows": partner}, device_id_type=pl.DeviceIdType.MESH)

    def chip_copy(k, hop):
        rows = pl.ds(pl.multiple_of(other(hop) * block, block), block)
        return pltpu.make_async_remote_copy(
            src_ref=half.at[k, rows], dst_ref=chip_in.at[k, hop - 1],
            send_sem=b_send.at[k, hop - 1], recv_sem=b_recv.at[k, hop - 1],
            device_id={"rows": other(hop) * CORES + core}, device_id_type=pl.DeviceIdType.MESH)

    @pl.when(step == 0)
    def _():
        barrier = pltpu.get_barrier_semaphore()
        pl.semaphore_signal(barrier, inc=1, device_id={"rows": partner},
                            device_id_type=pl.DeviceIdType.MESH)
        for hop in range(1, chips):
            pl.semaphore_signal(barrier, inc=1, device_id={"rows": other(hop) * CORES + core},
                                device_id_type=pl.DeviceIdType.MESH)
        pl.semaphore_wait(barrier, chips)

    @pl.when(step < chunks)
    def _():
        part[step] = (
            jnp.dot(first_ref[...], spec_ref[...], preferred_element_type=jnp.float32)
            + jnp.dot(second_ref[...], spec_ref[...], preferred_element_type=jnp.float32))
        core_copy(step).start()

    @pl.when(jnp.logical_and(step >= 1, step < chunks + 1))
    def _():
        k = step - 1
        core_copy(k).wait()
        rows = pl.ds(pl.multiple_of(core * half_rows, half_rows), half_rows)
        half[k] = part[k, rows] + core_in[k]
        for hop in range(1, chips):
            chip_copy(k, hop).start()

    @pl.when(step >= LAG)
    def _():
        k = step - LAG
        rows = pl.ds(pl.multiple_of(chip * block, block), block)
        for hop in range(1, chips):
            chip_copy(k, hop).wait()
        total = half[k, rows]
        for hop in range(1, chips):
            total = total + chip_in[k, hop - 1]
        out_ref[:, pl.ds(pl.multiple_of(k * width, width), width)] = total


def row_transform(spectra, first, second, count):
    depth = spectra.shape[0]
    width = 512
    chunks = NX // width
    chips = count // CORES
    half_rows = 2 * Y_WIN // CORES
    block = half_rows // chips
    whole = pl.BlockSpec((2 * Y_WIN, depth), lambda c: (0, 0))
    return pl.pallas_call(
        partial(row_kernel, count, chunks),
        out_shape=jax.ShapeDtypeStruct((block, NX), jnp.float32),
        grid=(chunks + LAG,),
        in_specs=[whole, whole,
                  pl.BlockSpec((depth, width), lambda c: (0, jnp.minimum(c, chunks - 1)))],
        out_specs=pl.BlockSpec((block, NX), lambda c: (0, 0)),
        scratch_shapes=[
            pltpu.VMEM((chunks, 2 * Y_WIN, width), jnp.float32),
            pltpu.VMEM((chunks, half_rows, width), jnp.float32),
            pltpu.VMEM((chunks, half_rows, width), jnp.float32),
            pltpu.VMEM((chunks, chips - 1, block, width), jnp.float32),
            pltpu.SemaphoreType.DMA((chunks,)),
            pltpu.SemaphoreType.DMA((chunks,)),
            pltpu.SemaphoreType.DMA((chunks, chips - 1)),
            pltpu.SemaphoreType.DMA((chunks, chips - 1)),
        ],
        compiler_params=pltpu.CompilerParams(
            collective_id=0, has_side_effects=True, vmem_limit_bytes=VMEM_BYTES),
    )(first, second, spectra)


def butterflies(real, imag):
    n = len(real)
    if n == 1:
        return real, imag
    even_r, even_i = butterflies(real[0::2], imag[0::2])
    odd_r, odd_i = butterflies(real[1::2], imag[1::2])
    out_r, out_i = [None] * n, [None] * n
    for k in range(n // 2):
        c, s = math.cos(2.0 * math.pi * k / n), math.sin(2.0 * math.pi * k / n)
        if k == 0:
            tr, ti = odd_r[k], odd_i[k]
        elif 4 * k == n:
            tr, ti = -odd_i[k], odd_r[k]
        else:
            tr, ti = odd_r[k] * c - odd_i[k] * s, odd_r[k] * s + odd_i[k] * c
        out_r[k], out_i[k] = even_r[k] + tr, even_i[k] + ti
        out_r[k + n // 2], out_i[k + n // 2] = even_r[k] - tr, even_i[k] - ti
    return out_r, out_i


def column_kernel(strip_ref, phase_ref, twist_ref, table_ref, pic_ref, power_ref, mid):
    band = strip_ref.shape[0] // 2

    @pl.loop(0, band // 8)
    def _(s):
        at = pl.multiple_of(s * 8, 8)
        real, imag = [], []
        for slab in range(SLABS):
            lanes = slice(slab * LANES, (slab + 1) * LANES)
            xr = strip_ref[pl.ds(at, 8), lanes]
            xi = strip_ref[pl.ds(band + at, 8), lanes]
            pc, ps = phase_ref[0:1, lanes], phase_ref[1:2, lanes]
            real.append(xr * pc - xi * ps)
            imag.append(xr * ps + xi * pc)
        real, imag = butterflies(real, imag)
        for slab in range(SLABS):
            tc, ts = twist_ref[0, slab:slab + 1, :], twist_ref[1, slab:slab + 1, :]
            mid[slab, pl.ds(at, 8), 0:LANES] = real[slab] * tc - imag[slab] * ts
            mid[slab, pl.ds(at, 8), LANES:2 * LANES] = real[slab] * ts + imag[slab] * tc

    per = 4

    @pl.loop(0, SLABS // per)
    def _(q):
        slabs = pl.ds(q * per, per)
        rows = mid[slabs].reshape(per * band, 2 * LANES)
        both = jnp.dot(rows, table_ref[...], precision=lax.Precision.HIGHEST,
                       preferred_element_type=jnp.float32)
        real, imag = both[:, :LANES], both[:, LANES:]
        pic_ref[0, slabs] = real.reshape(per, band, LANES)
        pic_ref[1, slabs] = imag.reshape(per, band, LANES)
        power_ref[slabs] = (real * real + imag * imag).reshape(per, band, LANES)


def column_transform(strip, phase):
    band = strip.shape[0] // 2
    lane = np.arange(LANES)
    twist = np.arange(SLABS)[:, None] * lane[None, :] * (2.0 * np.pi / NX)
    twist = np.stack([np.cos(twist), np.sin(twist)]).astype(np.float32)
    angle = lane[:, None] * lane[None, :] % LANES * (2.0 * np.pi / LANES)
    cosine, sine = np.cos(angle) / NX, np.sin(angle) / NX
    table = np.block([[cosine, sine], [-sine, cosine]]).astype(np.float32)
    return pl.pallas_call(
        column_kernel,
        out_shape=(jax.ShapeDtypeStruct((2, SLABS, band, LANES), jnp.float32),
                   jax.ShapeDtypeStruct((SLABS, band, LANES), jnp.float32)),
        scratch_shapes=[pltpu.VMEM((SLABS, band, 2 * LANES), jnp.float32)],
        compiler_params=pltpu.CompilerParams(vmem_limit_bytes=VMEM_BYTES),
    )(strip, phase, jnp.asarray(twist), jnp.asarray(table))


def wrapped(block, forward):
    lane = lax.broadcasted_iota(jnp.int32, block.shape, block.ndim - 1)
    shift = LANES - 1 if forward else 1
    edge = LANES - 1 if forward else 0
    return jnp.where(lane == edge, 0.0, pltpu.roll(block, shift, block.ndim - 1))


def focus_kernel(groups, count, smooth_ref, power_ref, pic_ref, order_ref, map_ref, field_ref,
                 rim, energy, score, send_s, send_q, send_r, recv_s, recv_q, recv_r,
                 halo_send, halo_recv, sends, recvs):
    band = power_ref.shape[1]
    strips = band // STRIP
    per = SLABS // groups
    piece = LANES // per
    width = groups * LANES
    place, me = lax.axis_index("rows"), lax.axis_index("depth")
    has_low, has_high = place > 0, place < count - 1

    def halo(kind):
        low = kind == 0
        return pltpu.make_async_remote_copy(
            src_ref=power_ref.at[:, pl.ds(0 if low else band - 8, 8)],
            dst_ref=rim.at[pl.ds(1, SLABS), pl.ds(8 + band if low else 0, 8)],
            send_sem=halo_send.at[kind], recv_sem=halo_recv.at[kind],
            device_id={"rows": lax.rem(place + (count - 1 if low else 1), count)},
            device_id_type=pl.DeviceIdType.MESH)

    def copies(s, hop):
        target = lax.rem(me + hop, per)
        return [pltpu.make_async_remote_copy(
            src_ref=src.at[s, target], dst_ref=dst.at[s, hop - 1],
            send_sem=sends.at[s, hop - 1, i], recv_sem=recvs.at[s, hop - 1, i],
            device_id={"depth": target}, device_id_type=pl.DeviceIdType.MESH)
            for i, (src, dst) in enumerate(
                ((send_s, recv_s), (send_q, recv_q), (send_r, recv_r)))]

    barrier = pltpu.get_barrier_semaphore()

    @pl.when(has_low)
    def _():
        pl.semaphore_signal(barrier, inc=1, device_id={"rows": place - 1},
                            device_id_type=pl.DeviceIdType.MESH)

    @pl.when(has_high)
    def _():
        pl.semaphore_signal(barrier, inc=1, device_id={"rows": place + 1},
                            device_id_type=pl.DeviceIdType.MESH)

    @pl.loop(1, per)
    def _(hop):
        pl.semaphore_signal(barrier, inc=1, device_id={"depth": lax.rem(me + hop, per)},
                            device_id_type=pl.DeviceIdType.MESH)

    pl.semaphore_wait(barrier, per - 1 + has_low.astype(jnp.int32) + has_high.astype(jnp.int32))

    @pl.when(has_low)
    def _():
        halo(0).start()

    @pl.when(has_high)
    def _():
        halo(1).start()

    rim[1:SLABS + 1, 8:8 + band, :] = power_ref[...]

    @pl.when(place == 0)
    def _():
        rim[1:SLABS + 1, 0:8, :] = jnp.zeros((SLABS, 8, LANES), jnp.float32)

    @pl.when(place == count - 1)
    def _():
        rim[1:SLABS + 1, 8 + band:16 + band, :] = jnp.zeros((SLABS, 8, LANES), jnp.float32)

    @pl.loop(0, strips)
    def _(turn):
        s = lax.rem(turn + 1, strips)
        at = pl.multiple_of(s * STRIP, STRIP)

        @pl.when(turn == max(strips - 2, 0))
        def _():
            @pl.when(has_low)
            def _():
                halo(0).wait_send()
                halo(1).wait_recv()

            @pl.when(has_high)
            def _():
                halo(1).wait_send()
                halo(0).wait_recv()

        window = pl.ds(at, STRIP + 16)
        rim[0, window, :] = wrapped(rim[SLABS, window, :], False)
        rim[SLABS + 1, window, :] = wrapped(rim[1, window, :], True)

        @pl.loop(0, SLABS)
        def _(slab):
            before, here, after = (rim[slab + j, window, :] for j in range(3))

            def vertical(x):
                return x[7:7 + STRIP] + 2.0 * x[8:8 + STRIP] + x[9:9 + STRIP]

            across = vertical(after) - vertical(before)
            horizontal = before + 2.0 * here + after
            downward = horizontal[9:9 + STRIP] - horizontal[7:7 + STRIP]
            energy[slab + MAXWIDTH] = across * across + downward * downward

        for k in range(MAXWIDTH):
            energy[k] = wrapped(energy[SLABS + k], False)
            energy[SLABS + MAXWIDTH + k] = wrapped(energy[MAXWIDTH + k], True)

        @pl.loop(0, SLABS)
        def _(slab):
            total = energy[slab + MAXWIDTH]
            for k in range(1, MAXWIDTH + 1):
                total = total + smooth_ref[0, k] * (
                    energy[slab + MAXWIDTH - k] + energy[slab + MAXWIDTH + k])
            score[slab] = smooth_ref[0, 4] * jnp.log(1.0 + total / smooth_ref[0, 0])

        block_of = lax.broadcasted_iota(jnp.int32, (STRIP, LANES), 1) // piece

        def exchanged(held):
            gap = 1
            while gap < per:
                low_lane = block_of // gap % 2 == 0
                for i in range(per):
                    if i // gap % 2 == 0:
                        a, c = held[i], held[i + gap]
                        held[i] = jnp.where(low_lane, a, pltpu.roll(c, gap * piece, 1))
                        held[i + gap] = jnp.where(
                            low_lane, pltpu.roll(a, LANES - gap * piece, 1), c)
                gap *= 2
            return held

        @pl.loop(0, groups)
        def _(g):
            lanes = pl.ds(pl.multiple_of(g * LANES, LANES), LANES)
            held = exchanged([score[g * per + i] for i in range(per)])
            for d in range(per):
                send_s[s, d, :, lanes] = held[d]
            real, imag = (
                exchanged([pic_ref[part, g * per + i, pl.ds(at, STRIP), :] for i in range(per)])
                for part in range(2))
            for d in range(per):
                largest = jnp.max(jnp.maximum(jnp.abs(real[d]), jnp.abs(imag[d])),
                                  axis=0, keepdims=True)
                largest = jnp.maximum(largest, TINY)
                send_r[s, d, :, lanes] = largest * (1.0 / STEPS)
                scale = STEPS / largest
                for part, value in ((0, real[d]), (1, imag[d])):
                    level = jnp.floor(value * scale + 0.5).astype(jnp.int32)
                    send_q[s, d, part * STRIP:(part + 1) * STRIP, lanes] = level.astype(jnp.int16)

        for d in range(per):
            send_r[s, d, :, width:width + LANES] = jnp.full((1, LANES), smooth_ref[0, 5])

        @pl.loop(1, per)
        def _(hop):
            for copy in copies(s, hop):
                copy.start()

        recv_s[s, per - 1] = send_s[s, me]
        recv_q[s, per - 1] = send_q[s, me]
        recv_r[s, per - 1] = send_r[s, me]

    @pl.loop(0, strips)
    def _(turn):
        s = lax.rem(turn + 1, strips)
        at = pl.multiple_of(s * STRIP, STRIP)

        @pl.loop(1, per)
        def _(hop):
            for copy in copies(s, hop):
                copy.wait()

        peak = recv_s[s, 0]
        for p in range(1, per):
            peak = jnp.maximum(peak, recv_s[s, p])
        summed = jnp.zeros_like(peak)
        totals = [jnp.zeros_like(peak) for _ in range(3)]
        for p in range(per):
            weight = jnp.exp(recv_s[s, p] - peak)
            summed = summed + weight
            totals[0] = totals[0] + weight * recv_r[s, p, :, width:width + 1]
            scaled = weight * recv_r[s, p, :, 0:width]
            for part in range(2):
                level = recv_q[s, p, part * STRIP:(part + 1) * STRIP, :]
                totals[1 + part] = totals[1 + part] + scaled * level.astype(jnp.int32).astype(
                    jnp.float32)
        merged = jnp.concatenate([total / summed for total in totals], axis=0)
        placed = jnp.zeros_like(merged)
        for _ in range(3):
            term = merged.astype(jnp.bfloat16)
            placed = placed + jnp.dot(term, order_ref[...], preferred_element_type=jnp.float32)
            merged = merged - term.astype(jnp.float32)
        rows = pl.ds(at, STRIP)
        map_ref[rows, :] = placed[0:STRIP]
        field_ref[0, rows, :] = placed[STRIP:2 * STRIP]
        field_ref[1, rows, :] = placed[2 * STRIP:3 * STRIP]


def focus(smooth, power, pic, targets, count):
    band = power.shape[1]
    strips = band // STRIP
    groups = SLABS // targets
    width = groups * LANES
    piece = LANES // targets
    spot = np.arange(width)
    slab = spot // LANES * targets + spot % LANES // piece
    order = np.zeros((width, width), np.float32)
    order[spot, spot % piece * SLABS + slab] = 1.0
    vmem = pl.BlockSpec(memory_space=pltpu.VMEM)
    records = [
        pltpu.VMEM((strips, targets, STRIP, width), jnp.float32),
        pltpu.VMEM((strips, targets, 2 * STRIP, width), jnp.int16),
        pltpu.VMEM((strips, targets, 1, width + LANES), jnp.float32),
    ]
    return pl.pallas_call(
        partial(focus_kernel, groups, count),
        out_shape=(jax.ShapeDtypeStruct((band, width), jnp.float32),
                   jax.ShapeDtypeStruct((2, band, width), jnp.float32)),
        in_specs=[pl.BlockSpec(memory_space=pltpu.SMEM), vmem, vmem, vmem],
        out_specs=(vmem, vmem),
        scratch_shapes=[
            pltpu.VMEM((SLABS + 2, band + 16, LANES), jnp.float32),
            pltpu.VMEM((SLABS + 2 * MAXWIDTH, STRIP, LANES), jnp.float32),
            pltpu.VMEM((SLABS, STRIP, LANES), jnp.float32),
            *records, *records,
            pltpu.SemaphoreType.DMA((2,)),
            pltpu.SemaphoreType.DMA((2,)),
            pltpu.SemaphoreType.DMA((strips, targets - 1, 3)),
            pltpu.SemaphoreType.DMA((strips, targets - 1, 3)),
        ],
        compiler_params=pltpu.CompilerParams(
            collective_id=1, has_side_effects=True, vmem_limit_bytes=VMEM_BYTES),
    )(smooth, power, pic, jnp.asarray(order, jnp.bfloat16))


def shards(spectrum, plane_index, kernel_width, focus_gain):
    count = lax.axis_size("rows")
    targets = lax.axis_size("depth")
    place = lax.axis_index("rows")
    plane, radius = plane_index[0], kernel_width[0]
    first, second = row_table(plane, place, count)
    spectra = spectrum.reshape(2 * spectrum.shape[1], NX)
    strip = row_transform(spectra, first, second, count)
    phase = line_phase(plane, jnp.arange(NX, dtype=jnp.int32))
    pic, power = column_transform(strip, jnp.stack([jnp.cos(phase), jnp.sin(phase)]))
    inside = (jnp.arange(1, MAXWIDTH + 1) <= radius).astype(jnp.float32)
    smooth = jnp.concatenate([
        (2 * radius + 1).astype(jnp.float32)[None], inside, focus_gain,
        plane_index.astype(jnp.float32) / DEPTHS])[None]
    return focus(smooth, power, pic, targets, count)


def solution(mesh):
    return jax.shard_map(
        shards,
        mesh=mesh,
        in_specs=(P(None, "rows", None), P("depth"), P("depth"), P("depth")),
        out_specs=(P("rows", "depth"), P(None, "rows", "depth")),
        check_vma=False,
    )
```

```python
from functools import partial
import math

import numpy as np
import jax
import jax.numpy as jnp
from jax import lax
from jax.experimental import pallas as pl
from jax.experimental.pallas import tpu as pltpu
from jax.sharding import PartitionSpec as P

NX = 4096
Y_WIN = 256
DEPTHS = 2048
MAXWIDTH = 3
LANES = 128
SLABS = NX // LANES
CORES = 2
UNIT = 1024
STRIP = 16
STEPS = 32767.0
TINY = 1e-33
VMEM_BYTES = 56 * 1024 * 1024


def line_phase(plane, freqs):
    signed = jnp.where(freqs < NX // 2, freqs, freqs - NX)
    square = signed * signed
    turns = (plane * (square % NX) + NX * (plane * (square // NX) % NX)) % (NX * NX)
    return turns.astype(jnp.float32) * (-2.0 * math.pi / (NX * NX))


def row_table(plane, place, count):
    freqs_n = NX // count
    band = Y_WIN // count
    turns = np.arange(Y_WIN)[:, None] * np.arange(freqs_n)[None, :] % NX
    angle = turns * (2.0 * np.pi / NX)
    base_cos = jnp.asarray(np.cos(angle).astype(np.float32))
    base_sin = jnp.asarray(np.sin(angle).astype(np.float32))
    phase = line_phase(plane, place * freqs_n + jnp.arange(freqs_n, dtype=jnp.int32))
    start = place * freqs_n * jnp.arange(Y_WIN, dtype=jnp.int32) % NX
    start_angle = start.astype(jnp.float32) * (2.0 * math.pi / NX)
    col_cos, col_sin = jnp.cos(phase)[None, :], jnp.sin(phase)[None, :]
    row_cos, row_sin = jnp.cos(start_angle)[:, None], jnp.sin(start_angle)[:, None]
    turn_cos = row_cos * col_cos - row_sin * col_sin
    turn_sin = row_cos * col_sin + row_sin * col_cos
    real = base_cos * turn_cos - base_sin * turn_sin
    imag = base_cos * turn_sin + base_sin * turn_cos
    upper = jnp.concatenate([real, -imag], axis=1)
    lower = jnp.concatenate([imag, real], axis=1)
    table = jnp.stack([upper, lower]).reshape(
        2, count // CORES, CORES, band // STRIP, STRIP, 2 * freqs_n)
    table = table.transpose(3, 2, 1, 0, 4, 5).reshape(band // STRIP, -1, 2 * freqs_n)
    first = lax.reduce_precision(table, 8, 7)
    return jnp.concatenate(
        [first.astype(jnp.bfloat16), (table - first).astype(jnp.bfloat16)], axis=1)


def butterflies(real, imag):
    n = len(real)
    if n == 1:
        return real, imag
    even_r, even_i = butterflies(real[0::2], imag[0::2])
    odd_r, odd_i = butterflies(real[1::2], imag[1::2])
    out_r, out_i = [None] * n, [None] * n
    for k in range(n // 2):
        c, s = math.cos(2.0 * math.pi * k / n), math.sin(2.0 * math.pi * k / n)
        if k == 0:
            tr, ti = odd_r[k], odd_i[k]
        elif 4 * k == n:
            tr, ti = -odd_i[k], odd_r[k]
        else:
            tr, ti = odd_r[k] * c - odd_i[k] * s, odd_r[k] * s + odd_i[k] * c
        out_r[k], out_i[k] = even_r[k] + tr, even_i[k] + ti
        out_r[k + n // 2], out_i[k + n // 2] = even_r[k] - tr, even_i[k] - ti
    return out_r, out_i


def wrapped(block, forward):
    lane = lax.broadcasted_iota(jnp.int32, block.shape, block.ndim - 1)
    shift = LANES - 1 if forward else 1
    edge = LANES - 1 if forward else 0
    return jnp.where(lane == edge, 0.0, pltpu.roll(block, shift, block.ndim - 1))


def kernel(count, smooth_ref, table_ref, phase_ref, twist_ref, dft_ref, order_ref, spec_ref,
           map_ref, field_ref, spec, part, core_in, half, chip_in, mid, pic, rim, energy, score,
           send_s, send_q, send_r, recv_s, recv_q, recv_r,
           loads, a_send, a_recv, b_send, b_recv, halo_send, halo_recv, sends, recvs):
    strips, targets, _, width = send_s.shape
    band = strips * STRIP
    groups = width // LANES
    piece = LANES // targets
    chips = count // CORES
    parts_n = NX // UNIT
    units = strips * parts_n
    half_rows = half.shape[1]
    block = 2 * STRIP
    place, me = lax.axis_index("rows"), lax.axis_index("depth")
    core, chip = lax.rem(place, CORES), lax.div(place, CORES)
    partner = chip * CORES + 1 - core
    has_low, has_high = place > 0, place < count - 1

    def load(c):
        return pltpu.make_async_copy(
            spec_ref.at[:, pl.ds(c * UNIT, UNIT)], spec.at[c], loads.at[c])

    def other(hop):
        return lax.rem(chip + hop, chips)

    def remote(src, dst, send, recv, target):
        return pltpu.make_async_remote_copy(
            src_ref=src, dst_ref=dst, send_sem=send, recv_sem=recv,
            device_id=target, device_id_type=pl.DeviceIdType.MESH)

    def core_copy(u):
        rows = pl.ds(pl.multiple_of((1 - core) * half_rows, half_rows), half_rows)
        return remote(part.at[u, rows], core_in.at[u], a_send.at[u], a_recv.at[u],
                      {"rows": partner})

    def chip_copy(u, hop):
        rows = pl.ds(pl.multiple_of(other(hop) * block, block), block)
        return remote(half.at[u, rows], chip_in.at[u, hop - 1], b_send.at[u, hop - 1],
                      b_recv.at[u, hop - 1], {"rows": other(hop) * CORES + core})

    def halo(kind):
        low = kind == 0
        own = pl.ds(8 if low else band, 8)
        there = pl.ds(8 + band if low else 0, 8)
        return remote(rim.at[pl.ds(1, SLABS), own], rim.at[pl.ds(1, SLABS), there],
                      halo_send.at[kind], halo_recv.at[kind],
                      {"rows": lax.rem(place + (count - 1 if low else 1), count)})

    def copies(s, hop):
        target = lax.rem(me + hop, targets)
        return [remote(src.at[s, target], dst.at[s, hop - 1], sends.at[s, hop - 1, i],
                       recvs.at[s, hop - 1, i], {"depth": target})
                for i, (src, dst) in enumerate(
                    ((send_s, recv_s), (send_q, recv_q), (send_r, recv_r)))]

    for c in range(parts_n):
        load(c).start()

    barrier = pltpu.get_barrier_semaphore()

    def greet(target):
        pl.semaphore_signal(barrier, inc=1, device_id=target,
                            device_id_type=pl.DeviceIdType.MESH)

    greet({"rows": partner})
    for hop in range(1, chips):
        greet({"rows": other(hop) * CORES + core})

    @pl.when(has_low)
    def _():
        greet({"rows": place - 1})

    @pl.when(has_high)
    def _():
        greet({"rows": place + 1})

    @pl.loop(1, targets)
    def _(hop):
        greet({"depth": lax.rem(me + hop, targets)})

    pl.semaphore_wait(barrier, chips + targets - 1 + has_low.astype(jnp.int32)
                      + has_high.astype(jnp.int32))

    @pl.when(place == 0)
    def _():
        rim[1:SLABS + 1, 0:8, :] = jnp.zeros((SLABS, 8, LANES), jnp.float32)

    @pl.when(place == count - 1)
    def _():
        rim[1:SLABS + 1, 8 + band:16 + band, :] = jnp.zeros((SLABS, 8, LANES), jnp.float32)

    def pass_on(u):
        core_copy(u).wait()
        rows = pl.ds(pl.multiple_of(core * half_rows, half_rows), half_rows)
        half[u] = part[u, rows] + core_in[u]
        for hop in range(1, chips):
            chip_copy(u, hop).start()

    @pl.loop(0, units)
    def _(u):
        strip, c = u // parts_n, u % parts_n

        @pl.when(u < parts_n)
        def _():
            load(u).wait()

        both = jnp.dot(table_ref[strip], spec[c], preferred_element_type=jnp.float32)
        part[u] = both[:CORES * half_rows] + both[CORES * half_rows:]
        core_copy(u).start()

        @pl.when(u >= 1)
        def _():
            pass_on(u - 1)

    pass_on(units - 1)

    def columns(k):
        for c in range(parts_n):
            for hop in range(1, chips):
                chip_copy(k * parts_n + c, hop).wait()

        @pl.loop(0, STRIP // 8)
        def _(s):
            at = pl.multiple_of(s * 8, 8)
            base = pl.multiple_of(chip * block + at, 8)
            real, imag = [], []
            for slab in range(SLABS):
                u = k * parts_n + slab * LANES // UNIT
                inner = slab * LANES % UNIT
                lanes = slice(inner, inner + LANES)

                def total(offset):
                    value = half[u, pl.ds(base + offset, 8), lanes]
                    for hop in range(1, chips):
                        value = value + chip_in[u, hop - 1, pl.ds(at + offset, 8), lanes]
                    return value

                xr, xi = total(0), total(STRIP)
                lanes = slice(slab * LANES, (slab + 1) * LANES)
                pc, ps = phase_ref[0:1, lanes], phase_ref[1:2, lanes]
                real.append(xr * pc - xi * ps)
                imag.append(xr * ps + xi * pc)
            real, imag = butterflies(real, imag)
            for slab in range(SLABS):
                tc, ts = twist_ref[0, slab:slab + 1, :], twist_ref[1, slab:slab + 1, :]
                mid[slab, pl.ds(at, 8), 0:LANES] = real[slab] * tc - imag[slab] * ts
                mid[slab, pl.ds(at, 8), LANES:2 * LANES] = real[slab] * ts + imag[slab] * tc

        per = 16
        at = pl.multiple_of(k * STRIP, STRIP)

        @pl.loop(0, SLABS // per)
        def _(q):
            slabs = pl.ds(q * per, per)
            rows = mid[slabs].reshape(per * STRIP, 2 * LANES)
            both = jnp.dot(rows, dft_ref[...], precision=lax.Precision.HIGHEST,
                           preferred_element_type=jnp.float32)
            real, imag = both[:, :LANES], both[:, LANES:]
            pic[0, slabs, pl.ds(at, STRIP)] = real.reshape(per, STRIP, LANES)
            pic[1, slabs, pl.ds(at, STRIP)] = imag.reshape(per, STRIP, LANES)
            rim[pl.ds(q * per + 1, per), pl.ds(at + 8, STRIP)] = (
                real * real + imag * imag).reshape(per, STRIP, LANES)

    def rows_of(g):
        return [pl.multiple_of(lax.rem(g * STRIP + band - 8, band), 8),
                pl.multiple_of(g * STRIP, 8)]

    def records(g):
        runs = rows_of(g)
        for n, run in enumerate(runs):
            window = pl.ds(run, 24)
            out = slice(8 * n, 8 * n + 8)
            rim[0, window, :] = wrapped(rim[SLABS, window, :], False)
            rim[SLABS + 1, window, :] = wrapped(rim[1, window, :], True)

            @pl.loop(0, SLABS)
            def _(slab):
                before, here, after = (rim[slab + j, window, :] for j in range(3))

                def vertical(x):
                    return x[7:15] + 2.0 * x[8:16] + x[9:17]

                across = vertical(after) - vertical(before)
                horizontal = before + 2.0 * here + after
                downward = horizontal[9:17] - horizontal[7:15]
                energy[slab + MAXWIDTH, out, :] = across * across + downward * downward

        for k in range(MAXWIDTH):
            energy[k] = wrapped(energy[SLABS + k], False)
            energy[SLABS + MAXWIDTH + k] = wrapped(energy[MAXWIDTH + k], True)

        @pl.loop(0, SLABS)
        def _(slab):
            total = energy[slab + MAXWIDTH]
            for k in range(1, MAXWIDTH + 1):
                total = total + smooth_ref[0, k] * (
                    energy[slab + MAXWIDTH - k] + energy[slab + MAXWIDTH + k])
            score[slab] = smooth_ref[0, 4] * jnp.log(1.0 + total / smooth_ref[0, 0])

        block_of = lax.broadcasted_iota(jnp.int32, (STRIP, LANES), 1) // piece

        def exchanged(held):
            gap = 1
            while gap < targets:
                low_lane = block_of // gap % 2 == 0
                for i in range(targets):
                    if i // gap % 2 == 0:
                        a, c = held[i], held[i + gap]
                        held[i] = jnp.where(low_lane, a, pltpu.roll(c, gap * piece, 1))
                        held[i + gap] = jnp.where(
                            low_lane, pltpu.roll(a, LANES - gap * piece, 1), c)
                gap *= 2
            return held

        @pl.loop(0, groups)
        def _(q):
            lanes = pl.ds(pl.multiple_of(q * LANES, LANES), LANES)
            held = exchanged([score[q * targets + i] for i in range(targets)])
            for d in range(targets):
                send_s[g, d, :, lanes] = held[d]
            real, imag = (
                exchanged([
                    jnp.concatenate([pic[kind, q * targets + i, pl.ds(run, 8), :]
                                     for run in runs], axis=0)
                    for i in range(targets)])
                for kind in range(2))
            for d in range(targets):
                largest = jnp.max(jnp.maximum(jnp.abs(real[d]), jnp.abs(imag[d])),
                                  axis=0, keepdims=True)
                largest = jnp.maximum(largest, TINY)
                send_r[g, d, :, lanes] = largest * (1.0 / STEPS)
                scale = STEPS / largest
                for kind, value in ((0, real[d]), (1, imag[d])):
                    level = jnp.floor(value * scale + 0.5).astype(jnp.int32)
                    send_q[g, d, kind * STRIP:(kind + 1) * STRIP, lanes] = level.astype(jnp.int16)

        for d in range(targets):
            send_r[g, d, :, width:width + LANES] = jnp.full((1, LANES), smooth_ref[0, 5])

        @pl.loop(1, targets)
        def _(hop):
            for copy in copies(g, hop):
                copy.start()

        recv_s[g, targets - 1] = send_s[g, me]
        recv_q[g, targets - 1] = send_q[g, me]
        recv_r[g, targets - 1] = send_r[g, me]

    @pl.loop(0, strips)
    def _(k):
        columns(k)

        @pl.when(jnp.logical_and(k == 0, has_low))
        def _():
            halo(0).start()

        @pl.when(jnp.logical_and(k == strips - 1, has_high))
        def _():
            halo(1).start()

        @pl.when(k == strips - 1)
        def _():
            @pl.when(has_low)
            def _():
                halo(0).wait_send()

            @pl.when(has_high)
            def _():
                halo(0).wait_recv()

        @pl.when(k >= 1)
        def _():
            records(k)

    @pl.when(has_high)
    def _():
        halo(1).wait_send()

    @pl.when(has_low)
    def _():
        halo(1).wait_recv()

    records(0)

    @pl.loop(0, strips)
    def _(turn):
        g = lax.rem(turn + 1, strips)

        @pl.loop(1, targets)
        def _(hop):
            for copy in copies(g, hop):
                copy.wait()

        peak = recv_s[g, 0]
        for p in range(1, targets):
            peak = jnp.maximum(peak, recv_s[g, p])
        summed = jnp.zeros_like(peak)
        totals = [jnp.zeros_like(peak) for _ in range(3)]
        for p in range(targets):
            weight = jnp.exp(recv_s[g, p] - peak)
            summed = summed + weight
            totals[0] = totals[0] + weight * recv_r[g, p, :, width:width + 1]
            scaled = weight * recv_r[g, p, :, 0:width]
            for kind in range(2):
                level = recv_q[g, p, kind * STRIP:(kind + 1) * STRIP, :]
                totals[1 + kind] = totals[1 + kind] + scaled * level.astype(jnp.int32).astype(
                    jnp.float32)
        merged = jnp.concatenate([total / summed for total in totals], axis=0)
        placed = jnp.zeros_like(merged)
        for _ in range(3):
            term = merged.astype(jnp.bfloat16)
            placed = placed + jnp.dot(term, order_ref[...], preferred_element_type=jnp.float32)
            merged = merged - term.astype(jnp.float32)
        for n, run in enumerate(rows_of(g)):
            rows = pl.ds(run, 8)
            map_ref[rows, :] = placed[8 * n:8 * n + 8]
            field_ref[0, rows, :] = placed[STRIP + 8 * n:STRIP + 8 * n + 8]
            field_ref[1, rows, :] = placed[2 * STRIP + 8 * n:2 * STRIP + 8 * n + 8]


def refocus(smooth, table, phase, spectra, count, targets):
    band = Y_WIN // count
    strips = band // STRIP
    groups = SLABS // targets
    width = groups * LANES
    piece = LANES // targets
    chips = count // CORES
    units = strips * NX // UNIT
    half_rows = chips * 2 * STRIP
    lane = np.arange(LANES)
    twist = np.arange(SLABS)[:, None] * lane[None, :] * (2.0 * np.pi / NX)
    twist = np.stack([np.cos(twist), np.sin(twist)]).astype(np.float32)
    angle = lane[:, None] * lane[None, :] % LANES * (2.0 * np.pi / LANES)
    cosine, sine = np.cos(angle) / NX, np.sin(angle) / NX
    dft = np.block([[cosine, sine], [-sine, cosine]]).astype(np.float32)
    spot = np.arange(width)
    slab = spot // LANES * targets + spot % LANES // piece
    order = np.zeros((width, width), np.float32)
    order[spot, spot % piece * SLABS + slab] = 1.0
    vmem = pl.BlockSpec(memory_space=pltpu.VMEM)
    records = [
        pltpu.VMEM((strips, targets, STRIP, width), jnp.float32),
        pltpu.VMEM((strips, targets, 2 * STRIP, width), jnp.int16),
        pltpu.VMEM((strips, targets, 1, width + LANES), jnp.float32),
    ]
    return pl.pallas_call(
        partial(kernel, count),
        out_shape=(jax.ShapeDtypeStruct((band, width), jnp.float32),
                   jax.ShapeDtypeStruct((2, band, width), jnp.float32)),
        in_specs=[pl.BlockSpec(memory_space=pltpu.SMEM)] + [vmem] * 5
        + [pl.BlockSpec(memory_space=pl.ANY)],
        out_specs=(vmem, vmem),
        scratch_shapes=[
            pltpu.VMEM((NX // UNIT, spectra.shape[0], UNIT), jnp.bfloat16),
            pltpu.VMEM((units, CORES * half_rows, UNIT), jnp.float32),
            pltpu.VMEM((units, half_rows, UNIT), jnp.float32),
            pltpu.VMEM((units, half_rows, UNIT), jnp.float32),
            pltpu.VMEM((units, chips - 1, 2 * STRIP, UNIT), jnp.float32),
            pltpu.VMEM((SLABS, STRIP, 2 * LANES), jnp.float32),
            pltpu.VMEM((2, SLABS, band, LANES), jnp.float32),
            pltpu.VMEM((SLABS + 2, band + 16, LANES), jnp.float32),
            pltpu.VMEM((SLABS + 2 * MAXWIDTH, STRIP, LANES), jnp.float32),
            pltpu.VMEM((SLABS, STRIP, LANES), jnp.float32),
            *records, *records,
            pltpu.SemaphoreType.DMA((NX // UNIT,)),
            pltpu.SemaphoreType.DMA((units,)),
            pltpu.SemaphoreType.DMA((units,)),
            pltpu.SemaphoreType.DMA((units, chips - 1)),
            pltpu.SemaphoreType.DMA((units, chips - 1)),
            pltpu.SemaphoreType.DMA((2,)),
            pltpu.SemaphoreType.DMA((2,)),
            pltpu.SemaphoreType.DMA((strips, targets - 1, 3)),
            pltpu.SemaphoreType.DMA((strips, targets - 1, 3)),
        ],
        compiler_params=pltpu.CompilerParams(
            collective_id=0, has_side_effects=True, vmem_limit_bytes=VMEM_BYTES),
    )(smooth, table, phase, jnp.asarray(twist), jnp.asarray(dft),
      jnp.asarray(order, jnp.bfloat16), spectra)


def shards(spectrum, plane_index, kernel_width, focus_gain):
    count = lax.axis_size("rows")
    targets = lax.axis_size("depth")
    place = lax.axis_index("rows")
    plane, radius = plane_index[0], kernel_width[0]
    table = row_table(plane, place, count)
    spectra = spectrum.reshape(2 * spectrum.shape[1], NX)
    phase = line_phase(plane, jnp.arange(NX, dtype=jnp.int32))
    phase = jnp.stack([jnp.cos(phase), jnp.sin(phase)])
    inside = (jnp.arange(1, MAXWIDTH + 1) <= radius).astype(jnp.float32)
    smooth = jnp.concatenate([
        (2 * radius + 1).astype(jnp.float32)[None], inside, focus_gain,
        plane_index.astype(jnp.float32) / DEPTHS])[None]
    return refocus(smooth, table, phase, spectra, count, targets)


def solution(mesh):
    return jax.shard_map(
        shards,
        mesh=mesh,
        in_specs=(P(None, "rows", None), P("depth"), P("depth"), P("depth")),
        out_specs=(P("rows", "depth"), P(None, "rows", "depth")),
        check_vma=False,
    )
```

```python
from functools import partial
import math

import numpy as np
import jax
import jax.numpy as jnp
from jax import lax
from jax.experimental import pallas as pl
from jax.experimental.pallas import tpu as pltpu
from jax.sharding import PartitionSpec as P

NX = 4096
Y_WIN = 256
DEPTHS = 2048
MAXWIDTH = 3
LANES = 128
SLABS = NX // LANES
CORES = 2
UNIT = 1024
STRIP = 16
STEPS = 32767.0
TINY = 1e-33
FINE_STEPS = 8388000.0
FINE_TINY = 1e-30
VMEM_BYTES = 56 * 1024 * 1024


def line_phase(plane, freqs):
    signed = jnp.where(freqs < NX // 2, freqs, freqs - NX)
    square = signed * signed
    turns = (plane * (square % NX) + NX * (plane * (square // NX) % NX)) % (NX * NX)
    return turns.astype(jnp.float32) * (-2.0 * math.pi / (NX * NX))


def row_table(plane, place, count):
    freqs_n = NX // count
    band = Y_WIN // count
    turns = np.arange(Y_WIN)[:, None] * np.arange(freqs_n)[None, :] % NX
    angle = turns * (2.0 * np.pi / NX)
    base_cos = jnp.asarray(np.cos(angle).astype(np.float32))
    base_sin = jnp.asarray(np.sin(angle).astype(np.float32))
    phase = line_phase(plane, place * freqs_n + jnp.arange(freqs_n, dtype=jnp.int32))
    start = place * freqs_n * jnp.arange(Y_WIN, dtype=jnp.int32) % NX
    start_angle = start.astype(jnp.float32) * (2.0 * math.pi / NX)
    col_cos, col_sin = jnp.cos(phase)[None, :], jnp.sin(phase)[None, :]
    row_cos, row_sin = jnp.cos(start_angle)[:, None], jnp.sin(start_angle)[:, None]
    turn_cos = row_cos * col_cos - row_sin * col_sin
    turn_sin = row_cos * col_sin + row_sin * col_cos
    real = base_cos * turn_cos - base_sin * turn_sin
    imag = base_cos * turn_sin + base_sin * turn_cos
    upper = jnp.concatenate([real, -imag], axis=1)
    lower = jnp.concatenate([imag, real], axis=1)
    table = jnp.stack([upper, lower]).reshape(
        2, count // CORES, CORES, band // STRIP, STRIP, 2 * freqs_n)
    table = table.transpose(3, 2, 1, 0, 4, 5).reshape(band // STRIP, -1, 2 * freqs_n)
    first = lax.reduce_precision(table, 8, 7)
    return jnp.concatenate(
        [first.astype(jnp.bfloat16), (table - first).astype(jnp.bfloat16)], axis=1)


def butterflies(real, imag):
    n = len(real)
    if n == 1:
        return real, imag
    even_r, even_i = butterflies(real[0::2], imag[0::2])
    odd_r, odd_i = butterflies(real[1::2], imag[1::2])
    out_r, out_i = [None] * n, [None] * n
    for k in range(n // 2):
        c, s = math.cos(2.0 * math.pi * k / n), math.sin(2.0 * math.pi * k / n)
        if k == 0:
            tr, ti = odd_r[k], odd_i[k]
        elif 4 * k == n:
            tr, ti = -odd_i[k], odd_r[k]
        else:
            tr, ti = odd_r[k] * c - odd_i[k] * s, odd_r[k] * s + odd_i[k] * c
        out_r[k], out_i[k] = even_r[k] + tr, even_i[k] + ti
        out_r[k + n // 2], out_i[k + n // 2] = even_r[k] - tr, even_i[k] - ti
    return out_r, out_i


def fine_code(value):
    largest = jnp.max(jnp.abs(value), axis=0, keepdims=True)
    largest = jnp.maximum(largest, FINE_TINY)
    level = jnp.floor(value * (FINE_STEPS / largest) + 0.5).astype(jnp.int32)
    upper = (level + 128) >> 8
    rest = level - (upper << 8)
    packed = jnp.maximum(rest[:STRIP], -127) * 256 + rest[STRIP:]
    return upper.astype(jnp.int16), packed.astype(jnp.int16), largest * (1.0 / FINE_STEPS)


def fine_value(upper, packed, unit):
    packed = packed.astype(jnp.int32)
    second = ((packed + 128) & 255) - 128
    rest = jnp.concatenate([(packed - second) >> 8, second], axis=0)
    return (upper.astype(jnp.int32) * 256 + rest).astype(jnp.float32) * unit


def wrapped(block, forward):
    lane = lax.broadcasted_iota(jnp.int32, block.shape, block.ndim - 1)
    shift = LANES - 1 if forward else 1
    edge = LANES - 1 if forward else 0
    return jnp.where(lane == edge, 0.0, pltpu.roll(block, shift, block.ndim - 1))


def kernel(count, smooth_ref, table_ref, phase_ref, twist_ref, dft_ref, order_ref, spec_ref,
           map_ref, field_ref, spec, part, core_in, half,
           code_out, unit_out, code_in, unit_in, strip_sum, mid, pic, rim, energy, score,
           send_s, send_q, send_r, recv_s, recv_q, recv_r,
           loads, a_send, a_recv, b_send, b_recv, halo_send, halo_recv, sends, recvs):
    strips, targets, _, width = send_s.shape
    band = strips * STRIP
    groups = width // LANES
    piece = LANES // targets
    chips = count // CORES
    parts_n = NX // UNIT
    units = strips * parts_n
    half_rows = half.shape[1]
    block = 2 * STRIP
    place, me = lax.axis_index("rows"), lax.axis_index("depth")
    core, chip = lax.rem(place, CORES), lax.div(place, CORES)
    partner = chip * CORES + 1 - core
    has_low, has_high = place > 0, place < count - 1

    def load(c):
        return pltpu.make_async_copy(
            spec_ref.at[:, pl.ds(c * UNIT, UNIT)], spec.at[c], loads.at[c])

    def other(hop):
        return lax.rem(chip + hop, chips)

    def remote(src, dst, send, recv, target):
        return pltpu.make_async_remote_copy(
            src_ref=src, dst_ref=dst, send_sem=send, recv_sem=recv,
            device_id=target, device_id_type=pl.DeviceIdType.MESH)

    def core_copy(u):
        rows = pl.ds(pl.multiple_of((1 - core) * half_rows, half_rows), half_rows)
        return remote(part.at[u, rows], core_in.at[u], a_send.at[u], a_recv.at[u],
                      {"rows": partner})

    def chip_copies(u, hop):
        return [remote(src.at[u, hop - 1], dst.at[u, hop - 1], b_send.at[u, hop - 1, i],
                       b_recv.at[u, hop - 1, i], {"rows": other(hop) * CORES + core})
                for i, (src, dst) in enumerate(((code_out, code_in), (unit_out, unit_in)))]

    def halo(kind):
        low = kind == 0
        own = pl.ds(8 if low else band, 8)
        there = pl.ds(8 + band if low else 0, 8)
        return remote(rim.at[pl.ds(1, SLABS), own], rim.at[pl.ds(1, SLABS), there],
                      halo_send.at[kind], halo_recv.at[kind],
                      {"rows": lax.rem(place + (count - 1 if low else 1), count)})

    def copies(s, hop):
        target = lax.rem(me + hop, targets)
        return [remote(src.at[s, target], dst.at[s, hop - 1], sends.at[s, hop - 1, i],
                       recvs.at[s, hop - 1, i], {"depth": target})
                for i, (src, dst) in enumerate(
                    ((send_s, recv_s), (send_q, recv_q), (send_r, recv_r)))]

    for c in range(parts_n):
        load(c).start()

    barrier = pltpu.get_barrier_semaphore()

    def greet(target):
        pl.semaphore_signal(barrier, inc=1, device_id=target,
                            device_id_type=pl.DeviceIdType.MESH)

    greet({"rows": partner})
    for hop in range(1, chips):
        greet({"rows": other(hop) * CORES + core})

    @pl.when(has_low)
    def _():
        greet({"rows": place - 1})

    @pl.when(has_high)
    def _():
        greet({"rows": place + 1})

    @pl.loop(1, targets)
    def _(hop):
        greet({"depth": lax.rem(me + hop, targets)})

    pl.semaphore_wait(barrier, chips + targets - 1 + has_low.astype(jnp.int32)
                      + has_high.astype(jnp.int32))

    @pl.when(place == 0)
    def _():
        rim[1:SLABS + 1, 0:8, :] = jnp.zeros((SLABS, 8, LANES), jnp.float32)

    @pl.when(place == count - 1)
    def _():
        rim[1:SLABS + 1, 8 + band:16 + band, :] = jnp.zeros((SLABS, 8, LANES), jnp.float32)

    def pass_on(u):
        core_copy(u).wait()
        rows = pl.ds(pl.multiple_of(core * half_rows, half_rows), half_rows)
        half[u] = part[u, rows] + core_in[u]
        for hop in range(1, chips):
            rows = pl.ds(pl.multiple_of(other(hop) * block, block), block)
            upper, packed, unit = fine_code(half[u, rows])
            code_out[u, hop - 1, 0:block, :] = upper
            code_out[u, hop - 1, block:block + STRIP, :] = packed
            unit_out[u, hop - 1] = unit
            for copy in chip_copies(u, hop):
                copy.start()

    @pl.loop(0, units)
    def _(u):
        strip, c = u // parts_n, u % parts_n

        @pl.when(u < parts_n)
        def _():
            load(u).wait()

        both = jnp.dot(table_ref[strip], spec[c], preferred_element_type=jnp.float32)
        part[u] = both[:CORES * half_rows] + both[CORES * half_rows:]
        core_copy(u).start()

        @pl.when(u >= 1)
        def _():
            pass_on(u - 1)

    pass_on(units - 1)

    def columns(k):
        rows = pl.ds(pl.multiple_of(chip * block, block), block)
        for c in range(parts_n):
            u = k * parts_n + c
            total = half[u, rows]
            for hop in range(1, chips):
                for copy in chip_copies(u, hop):
                    copy.wait()
                total = total + fine_value(
                    code_in[u, hop - 1, 0:block, :], code_in[u, hop - 1, block:block + STRIP, :],
                    unit_in[u, hop - 1])
            strip_sum[:, c * UNIT:(c + 1) * UNIT] = total

        @pl.loop(0, STRIP // 8)
        def _(s):
            at = pl.multiple_of(s * 8, 8)
            real, imag = [], []
            for slab in range(SLABS):
                lanes = slice(slab * LANES, (slab + 1) * LANES)
                xr = strip_sum[pl.ds(at, 8), lanes]
                xi = strip_sum[pl.ds(STRIP + at, 8), lanes]
                pc, ps = phase_ref[0:1, lanes], phase_ref[1:2, lanes]
                real.append(xr * pc - xi * ps)
                imag.append(xr * ps + xi * pc)
            real, imag = butterflies(real, imag)
            for slab in range(SLABS):
                tc, ts = twist_ref[0, slab:slab + 1, :], twist_ref[1, slab:slab + 1, :]
                mid[slab, pl.ds(at, 8), 0:LANES] = real[slab] * tc - imag[slab] * ts
                mid[slab, pl.ds(at, 8), LANES:2 * LANES] = real[slab] * ts + imag[slab] * tc

        per = 16
        at = pl.multiple_of(k * STRIP, STRIP)

        @pl.loop(0, SLABS // per)
        def _(q):
            slabs = pl.ds(q * per, per)
            rows = mid[slabs].reshape(per * STRIP, 2 * LANES)
            both = jnp.dot(rows, dft_ref[...], precision=lax.Precision.HIGHEST,
                           preferred_element_type=jnp.float32)
            real, imag = both[:, :LANES], both[:, LANES:]
            pic[0, slabs, pl.ds(at, STRIP)] = real.reshape(per, STRIP, LANES)
            pic[1, slabs, pl.ds(at, STRIP)] = imag.reshape(per, STRIP, LANES)
            rim[pl.ds(q * per + 1, per), pl.ds(at + 8, STRIP)] = (
                real * real + imag * imag).reshape(per, STRIP, LANES)

    def rows_of(g):
        return [pl.multiple_of(lax.rem(g * STRIP + band - 8, band), 8),
                pl.multiple_of(g * STRIP, 8)]

    def records(g):
        runs = rows_of(g)
        for n, run in enumerate(runs):
            window = pl.ds(run, 24)
            out = slice(8 * n, 8 * n + 8)
            rim[0, window, :] = wrapped(rim[SLABS, window, :], False)
            rim[SLABS + 1, window, :] = wrapped(rim[1, window, :], True)

            @pl.loop(0, SLABS)
            def _(slab):
                before, here, after = (rim[slab + j, window, :] for j in range(3))

                def vertical(x):
                    return x[7:15] + 2.0 * x[8:16] + x[9:17]

                across = vertical(after) - vertical(before)
                horizontal = before + 2.0 * here + after
                downward = horizontal[9:17] - horizontal[7:15]
                energy[slab + MAXWIDTH, out, :] = across * across + downward * downward

        for k in range(MAXWIDTH):
            energy[k] = wrapped(energy[SLABS + k], False)
            energy[SLABS + MAXWIDTH + k] = wrapped(energy[MAXWIDTH + k], True)

        @pl.loop(0, SLABS)
        def _(slab):
            total = energy[slab + MAXWIDTH]
            for k in range(1, MAXWIDTH + 1):
                total = total + smooth_ref[0, k] * (
                    energy[slab + MAXWIDTH - k] + energy[slab + MAXWIDTH + k])
            score[slab] = smooth_ref[0, 4] * jnp.log(1.0 + total / smooth_ref[0, 0])

        block_of = lax.broadcasted_iota(jnp.int32, (STRIP, LANES), 1) // piece

        def exchanged(held):
            gap = 1
            while gap < targets:
                low_lane = block_of // gap % 2 == 0
                for i in range(targets):
                    if i // gap % 2 == 0:
                        a, c = held[i], held[i + gap]
                        held[i] = jnp.where(low_lane, a, pltpu.roll(c, gap * piece, 1))
                        held[i + gap] = jnp.where(
                            low_lane, pltpu.roll(a, LANES - gap * piece, 1), c)
                gap *= 2
            return held

        @pl.loop(0, groups)
        def _(q):
            lanes = pl.ds(pl.multiple_of(q * LANES, LANES), LANES)
            held = exchanged([score[q * targets + i] for i in range(targets)])
            for d in range(targets):
                send_s[g, d, :, lanes] = held[d]
            real, imag = (
                exchanged([
                    jnp.concatenate([pic[kind, q * targets + i, pl.ds(run, 8), :]
                                     for run in runs], axis=0)
                    for i in range(targets)])
                for kind in range(2))
            for d in range(targets):
                largest = jnp.max(jnp.maximum(jnp.abs(real[d]), jnp.abs(imag[d])),
                                  axis=0, keepdims=True)
                largest = jnp.maximum(largest, TINY)
                send_r[g, d, :, lanes] = largest * (1.0 / STEPS)
                scale = STEPS / largest
                for kind, value in ((0, real[d]), (1, imag[d])):
                    level = jnp.floor(value * scale + 0.5).astype(jnp.int32)
                    send_q[g, d, kind * STRIP:(kind + 1) * STRIP, lanes] = level.astype(jnp.int16)

        for d in range(targets):
            send_r[g, d, :, width:width + LANES] = jnp.full((1, LANES), smooth_ref[0, 5])

        @pl.loop(1, targets)
        def _(hop):
            for copy in copies(g, hop):
                copy.start()

        recv_s[g, targets - 1] = send_s[g, me]
        recv_q[g, targets - 1] = send_q[g, me]
        recv_r[g, targets - 1] = send_r[g, me]

    @pl.loop(0, strips)
    def _(k):
        columns(k)

        @pl.when(jnp.logical_and(k == 0, has_low))
        def _():
            halo(0).start()

        @pl.when(jnp.logical_and(k == strips - 1, has_high))
        def _():
            halo(1).start()

        @pl.when(k == strips - 1)
        def _():
            @pl.when(has_low)
            def _():
                halo(0).wait_send()

            @pl.when(has_high)
            def _():
                halo(0).wait_recv()

        @pl.when(k >= 1)
        def _():
            records(k)

    @pl.when(has_high)
    def _():
        halo(1).wait_send()

    @pl.when(has_low)
    def _():
        halo(1).wait_recv()

    records(0)

    @pl.loop(0, strips)
    def _(turn):
        g = lax.rem(turn + 1, strips)

        @pl.loop(1, targets)
        def _(hop):
            for copy in copies(g, hop):
                copy.wait()

        peak = recv_s[g, 0]
        for p in range(1, targets):
            peak = jnp.maximum(peak, recv_s[g, p])
        summed = jnp.zeros_like(peak)
        totals = [jnp.zeros_like(peak) for _ in range(3)]
        for p in range(targets):
            weight = jnp.exp(recv_s[g, p] - peak)
            summed = summed + weight
            totals[0] = totals[0] + weight * recv_r[g, p, :, width:width + 1]
            scaled = weight * recv_r[g, p, :, 0:width]
            for kind in range(2):
                level = recv_q[g, p, kind * STRIP:(kind + 1) * STRIP, :]
                totals[1 + kind] = totals[1 + kind] + scaled * level.astype(jnp.int32).astype(
                    jnp.float32)
        merged = jnp.concatenate([total / summed for total in totals], axis=0)
        placed = jnp.zeros_like(merged)
        for _ in range(3):
            term = merged.astype(jnp.bfloat16)
            placed = placed + jnp.dot(term, order_ref[...], preferred_element_type=jnp.float32)
            merged = merged - term.astype(jnp.float32)
        for n, run in enumerate(rows_of(g)):
            rows = pl.ds(run, 8)
            map_ref[rows, :] = placed[8 * n:8 * n + 8]
            field_ref[0, rows, :] = placed[STRIP + 8 * n:STRIP + 8 * n + 8]
            field_ref[1, rows, :] = placed[2 * STRIP + 8 * n:2 * STRIP + 8 * n + 8]


def refocus(smooth, table, phase, spectra, count, targets):
    band = Y_WIN // count
    strips = band // STRIP
    groups = SLABS // targets
    width = groups * LANES
    piece = LANES // targets
    chips = count // CORES
    units = strips * NX // UNIT
    half_rows = chips * 2 * STRIP
    lane = np.arange(LANES)
    twist = np.arange(SLABS)[:, None] * lane[None, :] * (2.0 * np.pi / NX)
    twist = np.stack([np.cos(twist), np.sin(twist)]).astype(np.float32)
    angle = lane[:, None] * lane[None, :] % LANES * (2.0 * np.pi / LANES)
    cosine, sine = np.cos(angle) / NX, np.sin(angle) / NX
    dft = np.block([[cosine, sine], [-sine, cosine]]).astype(np.float32)
    spot = np.arange(width)
    slab = spot // LANES * targets + spot % LANES // piece
    order = np.zeros((width, width), np.float32)
    order[spot, spot % piece * SLABS + slab] = 1.0
    vmem = pl.BlockSpec(memory_space=pltpu.VMEM)
    codes = [
        pltpu.VMEM((units, chips - 1, 3 * STRIP, UNIT), jnp.int16),
        pltpu.VMEM((units, chips - 1, 1, UNIT), jnp.float32),
    ]
    records = [
        pltpu.VMEM((strips, targets, STRIP, width), jnp.float32),
        pltpu.VMEM((strips, targets, 2 * STRIP, width), jnp.int16),
        pltpu.VMEM((strips, targets, 1, width + LANES), jnp.float32),
    ]
    return pl.pallas_call(
        partial(kernel, count),
        out_shape=(jax.ShapeDtypeStruct((band, width), jnp.float32),
                   jax.ShapeDtypeStruct((2, band, width), jnp.float32)),
        in_specs=[pl.BlockSpec(memory_space=pltpu.SMEM)] + [vmem] * 5
        + [pl.BlockSpec(memory_space=pl.ANY)],
        out_specs=(vmem, vmem),
        scratch_shapes=[
            pltpu.VMEM((NX // UNIT, spectra.shape[0], UNIT), jnp.bfloat16),
            pltpu.VMEM((units, CORES * half_rows, UNIT), jnp.float32),
            pltpu.VMEM((units, half_rows, UNIT), jnp.float32),
            pltpu.VMEM((units, half_rows, UNIT), jnp.float32),
            *codes, *codes,
            pltpu.VMEM((2 * STRIP, NX), jnp.float32),
            pltpu.VMEM((SLABS, STRIP, 2 * LANES), jnp.float32),
            pltpu.VMEM((2, SLABS, band, LANES), jnp.float32),
            pltpu.VMEM((SLABS + 2, band + 16, LANES), jnp.float32),
            pltpu.VMEM((SLABS + 2 * MAXWIDTH, STRIP, LANES), jnp.float32),
            pltpu.VMEM((SLABS, STRIP, LANES), jnp.float32),
            *records, *records,
            pltpu.SemaphoreType.DMA((NX // UNIT,)),
            pltpu.SemaphoreType.DMA((units,)),
            pltpu.SemaphoreType.DMA((units,)),
            pltpu.SemaphoreType.DMA((units, chips - 1, 2)),
            pltpu.SemaphoreType.DMA((units, chips - 1, 2)),
            pltpu.SemaphoreType.DMA((2,)),
            pltpu.SemaphoreType.DMA((2,)),
            pltpu.SemaphoreType.DMA((strips, targets - 1, 3)),
            pltpu.SemaphoreType.DMA((strips, targets - 1, 3)),
        ],
        compiler_params=pltpu.CompilerParams(
            collective_id=0, has_side_effects=True, vmem_limit_bytes=VMEM_BYTES),
    )(smooth, table, phase, jnp.asarray(twist), jnp.asarray(dft),
      jnp.asarray(order, jnp.bfloat16), spectra)


def shards(spectrum, plane_index, kernel_width, focus_gain):
    count = lax.axis_size("rows")
    targets = lax.axis_size("depth")
    place = lax.axis_index("rows")
    plane, radius = plane_index[0], kernel_width[0]
    table = row_table(plane, place, count)
    spectra = spectrum.reshape(2 * spectrum.shape[1], NX)
    phase = line_phase(plane, jnp.arange(NX, dtype=jnp.int32))
    phase = jnp.stack([jnp.cos(phase), jnp.sin(phase)])
    inside = (jnp.arange(1, MAXWIDTH + 1) <= radius).astype(jnp.float32)
    smooth = jnp.concatenate([
        (2 * radius + 1).astype(jnp.float32)[None], inside, focus_gain,
        plane_index.astype(jnp.float32) / DEPTHS])[None]
    return refocus(smooth, table, phase, spectra, count, targets)


def solution(mesh):
    return jax.shard_map(
        shards,
        mesh=mesh,
        in_specs=(P(None, "rows", None), P("depth"), P("depth"), P("depth")),
        out_specs=(P("rows", "depth"), P(None, "rows", "depth")),
        check_vma=False,
    )
```

```python
from functools import partial
import math

import numpy as np
import jax
import jax.numpy as jnp
from jax import lax
from jax.experimental import pallas as pl
from jax.experimental.pallas import tpu as pltpu
from jax.sharding import PartitionSpec as P

NX = 4096
Y_WIN = 256
DEPTHS = 2048
MAXWIDTH = 3
LANES = 128
SLABS = NX // LANES
CORES = 2
UNIT = 1024
STRIP = 16
STEPS = 32767.0
TINY = 1e-33
FINE_STEPS = 8388000.0
FINE_TINY = 1e-30
VMEM_BYTES = 56 * 1024 * 1024


def line_phase(plane, freqs):
    signed = jnp.where(freqs < NX // 2, freqs, freqs - NX)
    square = signed * signed
    turns = (plane * (square % NX) + NX * (plane * (square // NX) % NX)) % (NX * NX)
    return turns.astype(jnp.float32) * (-2.0 * math.pi / (NX * NX))


def pair_of(band):
    return 2 if band // STRIP % 2 == 0 else 1


def row_table(plane, place, count):
    freqs_n = NX // count
    band = Y_WIN // count
    turns = np.arange(Y_WIN)[:, None] * np.arange(freqs_n)[None, :] % NX
    angle = turns * (2.0 * np.pi / NX)
    base_cos = jnp.asarray(np.cos(angle).astype(np.float32))
    base_sin = jnp.asarray(np.sin(angle).astype(np.float32))
    phase = line_phase(plane, place * freqs_n + jnp.arange(freqs_n, dtype=jnp.int32))
    start = place * freqs_n * jnp.arange(Y_WIN, dtype=jnp.int32) % NX
    start_angle = start.astype(jnp.float32) * (2.0 * math.pi / NX)
    col_cos, col_sin = jnp.cos(phase)[None, :], jnp.sin(phase)[None, :]
    row_cos, row_sin = jnp.cos(start_angle)[:, None], jnp.sin(start_angle)[:, None]
    turn_cos = row_cos * col_cos - row_sin * col_sin
    turn_sin = row_cos * col_sin + row_sin * col_cos
    real = base_cos * turn_cos - base_sin * turn_sin
    imag = base_cos * turn_sin + base_sin * turn_cos
    upper = jnp.concatenate([real, -imag], axis=1)
    lower = jnp.concatenate([imag, real], axis=1)
    table = jnp.stack([upper, lower]).reshape(
        2, count // CORES, CORES, band // STRIP, STRIP, 2 * freqs_n)
    table = table.transpose(3, 2, 1, 0, 4, 5)
    table = table.reshape(band // STRIP // pair_of(band), -1, 2 * freqs_n)
    first = lax.reduce_precision(table, 8, 7)
    return jnp.concatenate(
        [first.astype(jnp.bfloat16), (table - first).astype(jnp.bfloat16)], axis=1)


def butterflies(real, imag):
    n = len(real)
    if n == 1:
        return real, imag
    even_r, even_i = butterflies(real[0::2], imag[0::2])
    odd_r, odd_i = butterflies(real[1::2], imag[1::2])
    out_r, out_i = [None] * n, [None] * n
    for k in range(n // 2):
        c, s = math.cos(2.0 * math.pi * k / n), math.sin(2.0 * math.pi * k / n)
        if k == 0:
            tr, ti = odd_r[k], odd_i[k]
        elif 4 * k == n:
            tr, ti = -odd_i[k], odd_r[k]
        else:
            tr, ti = odd_r[k] * c - odd_i[k] * s, odd_r[k] * s + odd_i[k] * c
        out_r[k], out_i[k] = even_r[k] + tr, even_i[k] + ti
        out_r[k + n // 2], out_i[k + n // 2] = even_r[k] - tr, even_i[k] - ti
    return out_r, out_i


def fine_code(value):
    largest = jnp.max(jnp.abs(value), axis=0, keepdims=True)
    largest = jnp.maximum(largest, FINE_TINY)
    level = jnp.floor(value * (FINE_STEPS / largest) + 0.5).astype(jnp.int32)
    upper = (level + 128) >> 8
    rest = level - (upper << 8)
    packed = jnp.maximum(rest[:STRIP], -127) * 256 + rest[STRIP:]
    return upper.astype(jnp.int16), packed.astype(jnp.int16), largest * (1.0 / FINE_STEPS)


def fine_value(upper, packed, unit):
    packed = packed.astype(jnp.int32)
    second = ((packed + 128) & 255) - 128
    rest = jnp.concatenate([(packed - second) >> 8, second], axis=0)
    return (upper.astype(jnp.int32) * 256 + rest).astype(jnp.float32) * unit


def wrapped(block, forward):
    lane = lax.broadcasted_iota(jnp.int32, block.shape, block.ndim - 1)
    shift = LANES - 1 if forward else 1
    edge = LANES - 1 if forward else 0
    return jnp.where(lane == edge, 0.0, pltpu.roll(block, shift, block.ndim - 1))


def kernel(count, smooth_ref, table_ref, phase_ref, twist_ref, dft_ref, order_ref, spec_ref,
           map_ref, field_ref, spec, part, core_in, half,
           code_out, unit_out, code_in, unit_in, strip_sum, mid, pic, rim, energy, score,
           send_s, send_q, send_r, recv_s, recv_q, recv_r,
           loads, a_send, a_recv, b_send, b_recv, halo_send, halo_recv, sends, recvs):
    strips, targets, _, width = send_s.shape
    band = strips * STRIP
    groups = width // LANES
    piece = LANES // targets
    chips = count // CORES
    parts_n = NX // UNIT
    units = strips * parts_n
    half_rows = half.shape[1]
    block = 2 * STRIP
    place, me = lax.axis_index("rows"), lax.axis_index("depth")
    core, chip = lax.rem(place, CORES), lax.div(place, CORES)
    partner = chip * CORES + 1 - core
    has_low, has_high = place > 0, place < count - 1

    def load(c):
        return pltpu.make_async_copy(
            spec_ref.at[:, pl.ds(c * UNIT, UNIT)], spec.at[c], loads.at[c])

    def other(hop):
        return lax.rem(chip + hop, chips)

    def remote(src, dst, send, recv, target):
        return pltpu.make_async_remote_copy(
            src_ref=src, dst_ref=dst, send_sem=send, recv_sem=recv,
            device_id=target, device_id_type=pl.DeviceIdType.MESH)

    def core_copy(u):
        rows = pl.ds(pl.multiple_of((1 - core) * half_rows, half_rows), half_rows)
        return remote(part.at[u, rows], core_in.at[u], a_send.at[u], a_recv.at[u],
                      {"rows": partner})

    def chip_copies(u, hop):
        return [remote(src.at[u, hop - 1], dst.at[u, hop - 1], b_send.at[u, hop - 1, i],
                       b_recv.at[u, hop - 1, i], {"rows": other(hop) * CORES + core})
                for i, (src, dst) in enumerate(((code_out, code_in), (unit_out, unit_in)))]

    def halo(kind):
        low = kind == 0
        own = pl.ds(8 if low else band, 8)
        there = pl.ds(8 + band if low else 0, 8)
        return remote(rim.at[pl.ds(1, SLABS), own], rim.at[pl.ds(1, SLABS), there],
                      halo_send.at[kind], halo_recv.at[kind],
                      {"rows": lax.rem(place + (count - 1 if low else 1), count)})

    def copies(s, hop):
        target = lax.rem(me + hop, targets)
        return [remote(src.at[s, target], dst.at[s, hop - 1], sends.at[s, hop - 1, i],
                       recvs.at[s, hop - 1, i], {"depth": target})
                for i, (src, dst) in enumerate(
                    ((send_s, recv_s), (send_q, recv_q), (send_r, recv_r)))]

    for c in range(parts_n):
        load(c).start()

    barrier = pltpu.get_barrier_semaphore()

    def greet(target):
        pl.semaphore_signal(barrier, inc=1, device_id=target,
                            device_id_type=pl.DeviceIdType.MESH)

    greet({"rows": partner})
    for hop in range(1, chips):
        greet({"rows": other(hop) * CORES + core})

    @pl.when(has_low)
    def _():
        greet({"rows": place - 1})

    @pl.when(has_high)
    def _():
        greet({"rows": place + 1})

    @pl.loop(1, targets)
    def _(hop):
        greet({"depth": lax.rem(me + hop, targets)})

    pl.semaphore_wait(barrier, chips + targets - 1 + has_low.astype(jnp.int32)
                      + has_high.astype(jnp.int32))

    @pl.when(place == 0)
    def _():
        rim[1:SLABS + 1, 0:8, :] = jnp.zeros((SLABS, 8, LANES), jnp.float32)

    @pl.when(place == count - 1)
    def _():
        rim[1:SLABS + 1, 8 + band:16 + band, :] = jnp.zeros((SLABS, 8, LANES), jnp.float32)

    def pass_on(u):
        core_copy(u).wait()
        rows = pl.ds(pl.multiple_of(core * half_rows, half_rows), half_rows)
        half[u] = part[u, rows] + core_in[u]
        for hop in range(1, chips):
            rows = pl.ds(pl.multiple_of(other(hop) * block, block), block)
            upper, packed, unit = fine_code(half[u, rows])
            code_out[u, hop - 1, 0:block, :] = upper
            code_out[u, hop - 1, block:block + STRIP, :] = packed
            unit_out[u, hop - 1] = unit
            for copy in chip_copies(u, hop):
                copy.start()

    pair = pair_of(band)
    part_rows = CORES * half_rows

    def unit_of(p, c, i):
        return (p * pair + i) * parts_n + c

    def pass_all(p, c):
        for i in range(pair):
            pass_on(unit_of(p, c, i))

    def rows_transform(p):
        @pl.loop(0, parts_n)
        def _(c):
            @pl.when(p == 0)
            def _():
                load(c).wait()

            both = jnp.dot(table_ref[p], spec[c], preferred_element_type=jnp.float32)
            for i in range(pair):
                u = unit_of(p, c, i)
                low, high = i * part_rows, (pair + i) * part_rows
                part[u] = both[low:low + part_rows] + both[high:high + part_rows]
                core_copy(u).start()

            @pl.when(c >= 1)
            def _():
                pass_all(p, c - 1)

        pass_all(p, parts_n - 1)

    def columns(k):
        rows = pl.ds(pl.multiple_of(chip * block, block), block)
        for c in range(parts_n):
            u = k * parts_n + c
            total = half[u, rows]
            for hop in range(1, chips):
                for copy in chip_copies(u, hop):
                    copy.wait()
                total = total + fine_value(
                    code_in[u, hop - 1, 0:block, :], code_in[u, hop - 1, block:block + STRIP, :],
                    unit_in[u, hop - 1])
            strip_sum[:, c * UNIT:(c + 1) * UNIT] = total

        @pl.loop(0, STRIP // 8)
        def _(s):
            at = pl.multiple_of(s * 8, 8)
            real, imag = [], []
            for slab in range(SLABS):
                lanes = slice(slab * LANES, (slab + 1) * LANES)
                xr = strip_sum[pl.ds(at, 8), lanes]
                xi = strip_sum[pl.ds(STRIP + at, 8), lanes]
                pc, ps = phase_ref[0:1, lanes], phase_ref[1:2, lanes]
                real.append(xr * pc - xi * ps)
                imag.append(xr * ps + xi * pc)
            real, imag = butterflies(real, imag)
            for slab in range(SLABS):
                tc, ts = twist_ref[0, slab:slab + 1, :], twist_ref[1, slab:slab + 1, :]
                mid[slab, pl.ds(at, 8), 0:LANES] = real[slab] * tc - imag[slab] * ts
                mid[slab, pl.ds(at, 8), LANES:2 * LANES] = real[slab] * ts + imag[slab] * tc

        per = 16
        at = pl.multiple_of(k * STRIP, STRIP)

        @pl.loop(0, SLABS // per)
        def _(q):
            slabs = pl.ds(q * per, per)
            rows = mid[slabs].reshape(per * STRIP, 2 * LANES)
            both = jnp.dot(rows, dft_ref[...], precision=lax.Precision.HIGHEST,
                           preferred_element_type=jnp.float32)
            real, imag = both[:, :LANES], both[:, LANES:]
            pic[0, slabs, pl.ds(at, STRIP)] = real.reshape(per, STRIP, LANES)
            pic[1, slabs, pl.ds(at, STRIP)] = imag.reshape(per, STRIP, LANES)
            rim[pl.ds(q * per + 1, per), pl.ds(at + 8, STRIP)] = (
                real * real + imag * imag).reshape(per, STRIP, LANES)

    def rows_of(g):
        return [pl.multiple_of(lax.rem(g * STRIP + band - 8, band), 8),
                pl.multiple_of(g * STRIP, 8)]

    def records(g):
        runs = rows_of(g)
        for n, run in enumerate(runs):
            window = pl.ds(run, 24)
            out = slice(8 * n, 8 * n + 8)
            rim[0, window, :] = wrapped(rim[SLABS, window, :], False)
            rim[SLABS + 1, window, :] = wrapped(rim[1, window, :], True)

            @pl.loop(0, SLABS)
            def _(slab):
                before, here, after = (rim[slab + j, window, :] for j in range(3))

                def vertical(x):
                    return x[7:15] + 2.0 * x[8:16] + x[9:17]

                across = vertical(after) - vertical(before)
                horizontal = before + 2.0 * here + after
                downward = horizontal[9:17] - horizontal[7:15]
                energy[slab + MAXWIDTH, out, :] = across * across + downward * downward

        for k in range(MAXWIDTH):
            energy[k] = wrapped(energy[SLABS + k], False)
            energy[SLABS + MAXWIDTH + k] = wrapped(energy[MAXWIDTH + k], True)

        @pl.loop(0, SLABS)
        def _(slab):
            total = energy[slab + MAXWIDTH]
            for k in range(1, MAXWIDTH + 1):
                total = total + smooth_ref[0, k] * (
                    energy[slab + MAXWIDTH - k] + energy[slab + MAXWIDTH + k])
            score[slab] = smooth_ref[0, 4] * jnp.log(1.0 + total / smooth_ref[0, 0])

        block_of = lax.broadcasted_iota(jnp.int32, (STRIP, LANES), 1) // piece

        def exchanged(held):
            gap = 1
            while gap < targets:
                low_lane = block_of // gap % 2 == 0
                for i in range(targets):
                    if i // gap % 2 == 0:
                        a, c = held[i], held[i + gap]
                        held[i] = jnp.where(low_lane, a, pltpu.roll(c, gap * piece, 1))
                        held[i + gap] = jnp.where(
                            low_lane, pltpu.roll(a, LANES - gap * piece, 1), c)
                gap *= 2
            return held

        @pl.loop(0, groups)
        def _(q):
            lanes = pl.ds(pl.multiple_of(q * LANES, LANES), LANES)
            held = exchanged([score[q * targets + i] for i in range(targets)])
            for d in range(targets):
                send_s[g, d, :, lanes] = held[d]
            real, imag = (
                exchanged([
                    jnp.concatenate([pic[kind, q * targets + i, pl.ds(run, 8), :]
                                     for run in runs], axis=0)
                    for i in range(targets)])
                for kind in range(2))
            for d in range(targets):
                largest = jnp.max(jnp.maximum(jnp.abs(real[d]), jnp.abs(imag[d])),
                                  axis=0, keepdims=True)
                largest = jnp.maximum(largest, TINY)
                send_r[g, d, :, lanes] = largest * (1.0 / STEPS)
                scale = STEPS / largest
                for kind, value in ((0, real[d]), (1, imag[d])):
                    level = jnp.floor(value * scale + 0.5).astype(jnp.int32)
                    send_q[g, d, kind * STRIP:(kind + 1) * STRIP, lanes] = level.astype(jnp.int16)

        for d in range(targets):
            send_r[g, d, :, width:width + LANES] = jnp.full((1, LANES), smooth_ref[0, 5])

        @pl.loop(1, targets)
        def _(hop):
            for copy in copies(g, hop):
                copy.start()

        recv_s[g, targets - 1] = send_s[g, me]
        recv_q[g, targets - 1] = send_q[g, me]
        recv_r[g, targets - 1] = send_r[g, me]

    @pl.loop(0, strips)
    def _(k):
        @pl.when(k % pair == 0)
        def _():
            rows_transform(k // pair)

        columns(k)

        @pl.when(jnp.logical_and(k == 0, has_low))
        def _():
            halo(0).start()

        @pl.when(jnp.logical_and(k == strips - 1, has_high))
        def _():
            halo(1).start()

        @pl.when(k >= 1)
        def _():
            records(k)

    @pl.when(has_low)
    def _():
        halo(0).wait_send()

    @pl.when(has_high)
    def _():
        halo(0).wait_recv()

    @pl.when(has_high)
    def _():
        halo(1).wait_send()

    @pl.when(has_low)
    def _():
        halo(1).wait_recv()

    records(0)

    @pl.loop(0, strips)
    def _(turn):
        g = lax.rem(turn + 1, strips)

        @pl.loop(1, targets)
        def _(hop):
            for copy in copies(g, hop):
                copy.wait()

        peak = recv_s[g, 0]
        for p in range(1, targets):
            peak = jnp.maximum(peak, recv_s[g, p])
        summed = jnp.zeros_like(peak)
        totals = [jnp.zeros_like(peak) for _ in range(3)]
        for p in range(targets):
            weight = jnp.exp(recv_s[g, p] - peak)
            summed = summed + weight
            totals[0] = totals[0] + weight * recv_r[g, p, :, width:width + 1]
            scaled = weight * recv_r[g, p, :, 0:width]
            for kind in range(2):
                level = recv_q[g, p, kind * STRIP:(kind + 1) * STRIP, :]
                totals[1 + kind] = totals[1 + kind] + scaled * level.astype(jnp.int32).astype(
                    jnp.float32)
        merged = jnp.concatenate([total / summed for total in totals], axis=0)
        placed = jnp.zeros_like(merged)
        for _ in range(3):
            term = merged.astype(jnp.bfloat16)
            placed = placed + jnp.dot(term, order_ref[...], preferred_element_type=jnp.float32)
            merged = merged - term.astype(jnp.float32)
        for n, run in enumerate(rows_of(g)):
            rows = pl.ds(run, 8)
            map_ref[rows, :] = placed[8 * n:8 * n + 8]
            field_ref[0, rows, :] = placed[STRIP + 8 * n:STRIP + 8 * n + 8]
            field_ref[1, rows, :] = placed[2 * STRIP + 8 * n:2 * STRIP + 8 * n + 8]


def refocus(smooth, table, phase, spectra, count, targets):
    band = Y_WIN // count
    strips = band // STRIP
    groups = SLABS // targets
    width = groups * LANES
    piece = LANES // targets
    chips = count // CORES
    units = strips * NX // UNIT
    half_rows = chips * 2 * STRIP
    lane = np.arange(LANES)
    twist = np.arange(SLABS)[:, None] * lane[None, :] * (2.0 * np.pi / NX)
    twist = np.stack([np.cos(twist), np.sin(twist)]).astype(np.float32)
    angle = lane[:, None] * lane[None, :] % LANES * (2.0 * np.pi / LANES)
    cosine, sine = np.cos(angle) / NX, np.sin(angle) / NX
    dft = np.block([[cosine, sine], [-sine, cosine]]).astype(np.float32)
    spot = np.arange(width)
    slab = spot // LANES * targets + spot % LANES // piece
    order = np.zeros((width, width), np.float32)
    order[spot, spot % piece * SLABS + slab] = 1.0
    vmem = pl.BlockSpec(memory_space=pltpu.VMEM)
    codes = [
        pltpu.VMEM((units, chips - 1, 3 * STRIP, UNIT), jnp.int16),
        pltpu.VMEM((units, chips - 1, 1, UNIT), jnp.float32),
    ]
    records = [
        pltpu.VMEM((strips, targets, STRIP, width), jnp.float32),
        pltpu.VMEM((strips, targets, 2 * STRIP, width), jnp.int16),
        pltpu.VMEM((strips, targets, 1, width + LANES), jnp.float32),
    ]
    return pl.pallas_call(
        partial(kernel, count),
        out_shape=(jax.ShapeDtypeStruct((band, width), jnp.float32),
                   jax.ShapeDtypeStruct((2, band, width), jnp.float32)),
        in_specs=[pl.BlockSpec(memory_space=pltpu.SMEM)] + [vmem] * 5
        + [pl.BlockSpec(memory_space=pl.ANY)],
        out_specs=(vmem, vmem),
        scratch_shapes=[
            pltpu.VMEM((NX // UNIT, spectra.shape[0], UNIT), jnp.bfloat16),
            pltpu.VMEM((units, CORES * half_rows, UNIT), jnp.float32),
            pltpu.VMEM((units, half_rows, UNIT), jnp.float32),
            pltpu.VMEM((units, half_rows, UNIT), jnp.float32),
            *codes, *codes,
            pltpu.VMEM((2 * STRIP, NX), jnp.float32),
            pltpu.VMEM((SLABS, STRIP, 2 * LANES), jnp.float32),
            pltpu.VMEM((2, SLABS, band, LANES), jnp.float32),
            pltpu.VMEM((SLABS + 2, band + 16, LANES), jnp.float32),
            pltpu.VMEM((SLABS + 2 * MAXWIDTH, STRIP, LANES), jnp.float32),
            pltpu.VMEM((SLABS, STRIP, LANES), jnp.float32),
            *records, *records,
            pltpu.SemaphoreType.DMA((NX // UNIT,)),
            pltpu.SemaphoreType.DMA((units,)),
            pltpu.SemaphoreType.DMA((units,)),
            pltpu.SemaphoreType.DMA((units, chips - 1, 2)),
            pltpu.SemaphoreType.DMA((units, chips - 1, 2)),
            pltpu.SemaphoreType.DMA((2,)),
            pltpu.SemaphoreType.DMA((2,)),
            pltpu.SemaphoreType.DMA((strips, targets - 1, 3)),
            pltpu.SemaphoreType.DMA((strips, targets - 1, 3)),
        ],
        compiler_params=pltpu.CompilerParams(
            collective_id=0, has_side_effects=True, vmem_limit_bytes=VMEM_BYTES),
    )(smooth, table, phase, jnp.asarray(twist), jnp.asarray(dft),
      jnp.asarray(order, jnp.bfloat16), spectra)


def shards(spectrum, plane_index, kernel_width, focus_gain):
    count = lax.axis_size("rows")
    targets = lax.axis_size("depth")
    place = lax.axis_index("rows")
    plane, radius = plane_index[0], kernel_width[0]
    table = row_table(plane, place, count)
    spectra = spectrum.reshape(2 * spectrum.shape[1], NX)
    phase = line_phase(plane, jnp.arange(NX, dtype=jnp.int32))
    phase = jnp.stack([jnp.cos(phase), jnp.sin(phase)])
    inside = (jnp.arange(1, MAXWIDTH + 1) <= radius).astype(jnp.float32)
    smooth = jnp.concatenate([
        (2 * radius + 1).astype(jnp.float32)[None], inside, focus_gain,
        plane_index.astype(jnp.float32) / DEPTHS])[None]
    return refocus(smooth, table, phase, spectra, count, targets)


def solution(mesh):
    return jax.shard_map(
        shards,
        mesh=mesh,
        in_specs=(P(None, "rows", None), P("depth"), P("depth"), P("depth")),
        out_specs=(P("rows", "depth"), P(None, "rows", "depth")),
        check_vma=False,
    )
```

```python
from functools import partial
import math

import numpy as np
import jax
import jax.numpy as jnp
from jax import lax
from jax.experimental import pallas as pl
from jax.experimental.pallas import tpu as pltpu
from jax.sharding import PartitionSpec as P

NX = 4096
Y_WIN = 256
DEPTHS = 2048
MAXWIDTH = 3
LANES = 128
SLABS = NX // LANES
CORES = 2
UNIT = 1024
STRIP = 16
STEPS = 32767.0
TINY = 1e-33
FINE_STEPS = 8388000.0
FINE_TINY = 1e-30
VMEM_BYTES = 56 * 1024 * 1024


def line_phase(plane, freqs):
    signed = jnp.where(freqs < NX // 2, freqs, freqs - NX)
    square = signed * signed
    turns = (plane * (square % NX) + NX * (plane * (square // NX) % NX)) % (NX * NX)
    return turns.astype(jnp.float32) * (-2.0 * math.pi / (NX * NX))


def pair_of(band):
    return 2 if band // STRIP % 2 == 0 else 1


def row_order(values, count):
    band = Y_WIN // count
    split = values.reshape(count // CORES, CORES, band // STRIP, STRIP, -1)
    return split.transpose(2, 1, 0, 3, 4).reshape(Y_WIN, -1)


def row_phases(plane, place, count):
    freqs_n = NX // count
    turns = np.arange(Y_WIN)[:, None] * np.arange(freqs_n)[None, :] % NX
    angle = row_order(turns * (2.0 * np.pi / NX), count)
    base = np.stack([np.cos(angle), np.sin(angle)]).astype(np.float32)
    phase = line_phase(plane, place * freqs_n + jnp.arange(freqs_n, dtype=jnp.int32))
    rows = row_order(np.arange(Y_WIN, dtype=np.int32), count)
    start = (place * freqs_n * jnp.asarray(rows) % NX).astype(jnp.float32)
    start = start * (2.0 * math.pi / NX)
    return (jnp.asarray(base), jnp.stack([jnp.cos(phase), jnp.sin(phase)]),
            jnp.stack([jnp.cos(start), jnp.sin(start)]))


def butterflies(real, imag):
    n = len(real)
    if n == 1:
        return real, imag
    even_r, even_i = butterflies(real[0::2], imag[0::2])
    odd_r, odd_i = butterflies(real[1::2], imag[1::2])
    out_r, out_i = [None] * n, [None] * n
    for k in range(n // 2):
        c, s = math.cos(2.0 * math.pi * k / n), math.sin(2.0 * math.pi * k / n)
        if k == 0:
            tr, ti = odd_r[k], odd_i[k]
        elif 4 * k == n:
            tr, ti = -odd_i[k], odd_r[k]
        else:
            tr, ti = odd_r[k] * c - odd_i[k] * s, odd_r[k] * s + odd_i[k] * c
        out_r[k], out_i[k] = even_r[k] + tr, even_i[k] + ti
        out_r[k + n // 2], out_i[k + n // 2] = even_r[k] - tr, even_i[k] - ti
    return out_r, out_i


def fine_code(value):
    largest = jnp.max(jnp.abs(value), axis=0, keepdims=True)
    largest = jnp.maximum(largest, FINE_TINY)
    level = jnp.floor(value * (FINE_STEPS / largest) + 0.5).astype(jnp.int32)
    upper = (level + 128) >> 8
    rest = level - (upper << 8)
    packed = jnp.maximum(rest[:STRIP], -127) * 256 + rest[STRIP:]
    return upper.astype(jnp.int16), packed.astype(jnp.int16), largest * (1.0 / FINE_STEPS)


def fine_value(upper, packed, unit):
    packed = packed.astype(jnp.int32)
    second = ((packed + 128) & 255) - 128
    rest = jnp.concatenate([(packed - second) >> 8, second], axis=0)
    return (upper.astype(jnp.int32) * 256 + rest).astype(jnp.float32) * unit


def wrapped(block, forward):
    lane = lax.broadcasted_iota(jnp.int32, block.shape, block.ndim - 1)
    shift = LANES - 1 if forward else 1
    edge = LANES - 1 if forward else 0
    return jnp.where(lane == edge, 0.0, pltpu.roll(block, shift, block.ndim - 1))


def kernel(count, smooth_ref, base_ref, turn_ref, start_ref, phase_ref, twist_ref, dft_ref, order_ref, spec_ref,
           map_ref, field_ref, table, spec, part, core_in, half,
           code_out, unit_out, code_in, unit_in, strip_sum, mid, pic, rim, energy, score,
           send_s, send_q, send_r, recv_s, recv_q, recv_r,
           loads, a_send, a_recv, b_send, b_recv, halo_send, halo_recv, sends, recvs):
    strips, targets, _, width = send_s.shape
    band = strips * STRIP
    groups = width // LANES
    piece = LANES // targets
    chips = count // CORES
    parts_n = NX // UNIT
    units = strips * parts_n
    half_rows = half.shape[1]
    block = 2 * STRIP
    place, me = lax.axis_index("rows"), lax.axis_index("depth")
    core, chip = lax.rem(place, CORES), lax.div(place, CORES)
    partner = chip * CORES + 1 - core
    has_low, has_high = place > 0, place < count - 1

    def load(c):
        return pltpu.make_async_copy(
            spec_ref.at[:, pl.ds(c * UNIT, UNIT)], spec.at[c], loads.at[c])

    def other(hop):
        return lax.rem(chip + hop, chips)

    def remote(src, dst, send, recv, target):
        return pltpu.make_async_remote_copy(
            src_ref=src, dst_ref=dst, send_sem=send, recv_sem=recv,
            device_id=target, device_id_type=pl.DeviceIdType.MESH)

    def core_copy(u):
        rows = pl.ds(pl.multiple_of((1 - core) * half_rows, half_rows), half_rows)
        return remote(part.at[u, rows], core_in.at[u], a_send.at[u], a_recv.at[u],
                      {"rows": partner})

    def chip_copies(u, hop):
        return [remote(src.at[u, hop - 1], dst.at[u, hop - 1], b_send.at[u, hop - 1, i],
                       b_recv.at[u, hop - 1, i], {"rows": other(hop) * CORES + core})
                for i, (src, dst) in enumerate(((code_out, code_in), (unit_out, unit_in)))]

    def halo(kind):
        low = kind == 0
        own = pl.ds(8 if low else band, 8)
        there = pl.ds(8 + band if low else 0, 8)
        return remote(rim.at[pl.ds(1, SLABS), own], rim.at[pl.ds(1, SLABS), there],
                      halo_send.at[kind], halo_recv.at[kind],
                      {"rows": lax.rem(place + (count - 1 if low else 1), count)})

    def copies(s, hop):
        target = lax.rem(me + hop, targets)
        return [remote(src.at[s, target], dst.at[s, hop - 1], sends.at[s, hop - 1, i],
                       recvs.at[s, hop - 1, i], {"depth": target})
                for i, (src, dst) in enumerate(
                    ((send_s, recv_s), (send_q, recv_q), (send_r, recv_r)))]

    for c in range(parts_n):
        load(c).start()

    barrier = pltpu.get_barrier_semaphore()

    def greet(target):
        pl.semaphore_signal(barrier, inc=1, device_id=target,
                            device_id_type=pl.DeviceIdType.MESH)

    greet({"rows": partner})
    for hop in range(1, chips):
        greet({"rows": other(hop) * CORES + core})

    @pl.when(has_low)
    def _():
        greet({"rows": place - 1})

    @pl.when(has_high)
    def _():
        greet({"rows": place + 1})

    @pl.loop(1, targets)
    def _(hop):
        greet({"depth": lax.rem(me + hop, targets)})

    pl.semaphore_wait(barrier, chips + targets - 1 + has_low.astype(jnp.int32)
                      + has_high.astype(jnp.int32))

    @pl.when(place == 0)
    def _():
        rim[1:SLABS + 1, 0:8, :] = jnp.zeros((SLABS, 8, LANES), jnp.float32)

    @pl.when(place == count - 1)
    def _():
        rim[1:SLABS + 1, 8 + band:16 + band, :] = jnp.zeros((SLABS, 8, LANES), jnp.float32)

    def pass_on(u):
        core_copy(u).wait()
        rows = pl.ds(pl.multiple_of(core * half_rows, half_rows), half_rows)
        half[u] = part[u, rows] + core_in[u]
        for hop in range(1, chips):
            rows = pl.ds(pl.multiple_of(other(hop) * block, block), block)
            upper, packed, unit = fine_code(half[u, rows])
            code_out[u, hop - 1, 0:block, :] = upper
            code_out[u, hop - 1, block:block + STRIP, :] = packed
            unit_out[u, hop - 1] = unit
            for copy in chip_copies(u, hop):
                copy.start()

    pair = pair_of(band)
    part_rows = CORES * half_rows

    def unit_of(p, c, i):
        return (p * pair + i) * parts_n + c

    def pass_all(p, c):
        for i in range(pair):
            pass_on(unit_of(p, c, i))

    def make_table(p):
        blocks = pair * CORES * chips
        freqs_n = turn_ref.shape[1]
        pc, ps = turn_ref[0:1, :], turn_ref[1:2, :]

        @pl.loop(0, blocks)
        def _(b):
            rows = pl.ds(pl.multiple_of((p * blocks + b) * STRIP, STRIP), STRIP)
            bc, bs = base_ref[0, rows, :], base_ref[1, rows, :]
            rc, rs = start_ref[0, rows, :], start_ref[1, rows, :]
            tc, ts = rc * pc - rs * ps, rc * ps + rs * pc
            real, imag = bc * tc - bs * ts, bc * ts + bs * tc
            at = pl.multiple_of(b * block, block)
            for value, places in ((real, ((0, 0), (STRIP, freqs_n))),
                                  (imag, ((STRIP, 0),)), (-imag, ((0, freqs_n),))):
                first = value.astype(jnp.bfloat16)
                second = (value - first.astype(jnp.float32)).astype(jnp.bfloat16)
                for row, lane in places:
                    lanes = slice(lane, lane + freqs_n)
                    table[p, pl.ds(at + row, STRIP), lanes] = first
                    table[p, pl.ds(at + row + blocks * block, STRIP), lanes] = second

    def rows_transform(p):
        make_table(p)

        @pl.loop(0, parts_n)
        def _(c):
            @pl.when(p == 0)
            def _():
                load(c).wait()

            both = jnp.dot(table[p], spec[c], preferred_element_type=jnp.float32)
            for i in range(pair):
                u = unit_of(p, c, i)
                low, high = i * part_rows, (pair + i) * part_rows
                part[u] = both[low:low + part_rows] + both[high:high + part_rows]
                core_copy(u).start()

            @pl.when(c >= 1)
            def _():
                pass_all(p, c - 1)

        pass_all(p, parts_n - 1)

    @pl.loop(0, strips // pair)
    def _(p):
        rows_transform(p)

    def columns(k):
        rows = pl.ds(pl.multiple_of(chip * block, block), block)
        for c in range(parts_n):
            u = k * parts_n + c
            total = half[u, rows]
            for hop in range(1, chips):
                for copy in chip_copies(u, hop):
                    copy.wait()
                total = total + fine_value(
                    code_in[u, hop - 1, 0:block, :], code_in[u, hop - 1, block:block + STRIP, :],
                    unit_in[u, hop - 1])
            strip_sum[:, c * UNIT:(c + 1) * UNIT] = total

        @pl.loop(0, STRIP // 8)
        def _(s):
            at = pl.multiple_of(s * 8, 8)
            real, imag = [], []
            for slab in range(SLABS):
                lanes = slice(slab * LANES, (slab + 1) * LANES)
                xr = strip_sum[pl.ds(at, 8), lanes]
                xi = strip_sum[pl.ds(STRIP + at, 8), lanes]
                pc, ps = phase_ref[0:1, lanes], phase_ref[1:2, lanes]
                real.append(xr * pc - xi * ps)
                imag.append(xr * ps + xi * pc)
            real, imag = butterflies(real, imag)
            for slab in range(SLABS):
                tc, ts = twist_ref[0, slab:slab + 1, :], twist_ref[1, slab:slab + 1, :]
                mid[slab, pl.ds(at, 8), 0:LANES] = real[slab] * tc - imag[slab] * ts
                mid[slab, pl.ds(at, 8), LANES:2 * LANES] = real[slab] * ts + imag[slab] * tc

        per = 16
        at = pl.multiple_of(k * STRIP, STRIP)

        @pl.loop(0, SLABS // per)
        def _(q):
            slabs = pl.ds(q * per, per)
            rows = mid[slabs].reshape(per * STRIP, 2 * LANES)
            both = jnp.dot(rows, dft_ref[...], precision=lax.Precision.HIGHEST,
                           preferred_element_type=jnp.float32)
            real, imag = both[:, :LANES], both[:, LANES:]
            pic[0, slabs, pl.ds(at, STRIP)] = real.reshape(per, STRIP, LANES)
            pic[1, slabs, pl.ds(at, STRIP)] = imag.reshape(per, STRIP, LANES)
            rim[pl.ds(q * per + 1, per), pl.ds(at + 8, STRIP)] = (
                real * real + imag * imag).reshape(per, STRIP, LANES)

    def rows_of(g):
        return [pl.multiple_of(lax.rem(g * STRIP + band - 8, band), 8),
                pl.multiple_of(g * STRIP, 8)]

    def records(g):
        runs = rows_of(g)
        for n, run in enumerate(runs):
            window = pl.ds(run, 24)
            out = slice(8 * n, 8 * n + 8)
            rim[0, window, :] = wrapped(rim[SLABS, window, :], False)
            rim[SLABS + 1, window, :] = wrapped(rim[1, window, :], True)

            @pl.loop(0, SLABS)
            def _(slab):
                before, here, after = (rim[slab + j, window, :] for j in range(3))

                def vertical(x):
                    return x[7:15] + 2.0 * x[8:16] + x[9:17]

                across = vertical(after) - vertical(before)
                horizontal = before + 2.0 * here + after
                downward = horizontal[9:17] - horizontal[7:15]
                energy[slab + MAXWIDTH, out, :] = across * across + downward * downward

        for k in range(MAXWIDTH):
            energy[k] = wrapped(energy[SLABS + k], False)
            energy[SLABS + MAXWIDTH + k] = wrapped(energy[MAXWIDTH + k], True)

        @pl.loop(0, SLABS)
        def _(slab):
            total = energy[slab + MAXWIDTH]
            for k in range(1, MAXWIDTH + 1):
                total = total + smooth_ref[0, k] * (
                    energy[slab + MAXWIDTH - k] + energy[slab + MAXWIDTH + k])
            score[slab] = smooth_ref[0, 4] * jnp.log(1.0 + total / smooth_ref[0, 0])

        block_of = lax.broadcasted_iota(jnp.int32, (STRIP, LANES), 1) // piece

        def exchanged(held):
            gap = 1
            while gap < targets:
                low_lane = block_of // gap % 2 == 0
                for i in range(targets):
                    if i // gap % 2 == 0:
                        a, c = held[i], held[i + gap]
                        held[i] = jnp.where(low_lane, a, pltpu.roll(c, gap * piece, 1))
                        held[i + gap] = jnp.where(
                            low_lane, pltpu.roll(a, LANES - gap * piece, 1), c)
                gap *= 2
            return held

        @pl.loop(0, groups)
        def _(q):
            lanes = pl.ds(pl.multiple_of(q * LANES, LANES), LANES)
            held = exchanged([score[q * targets + i] for i in range(targets)])
            for d in range(targets):
                send_s[g, d, :, lanes] = held[d]
            real, imag = (
                exchanged([
                    jnp.concatenate([pic[kind, q * targets + i, pl.ds(run, 8), :]
                                     for run in runs], axis=0)
                    for i in range(targets)])
                for kind in range(2))
            for d in range(targets):
                largest = jnp.max(jnp.maximum(jnp.abs(real[d]), jnp.abs(imag[d])),
                                  axis=0, keepdims=True)
                largest = jnp.maximum(largest, TINY)
                send_r[g, d, :, lanes] = largest * (1.0 / STEPS)
                scale = STEPS / largest
                for kind, value in ((0, real[d]), (1, imag[d])):
                    level = jnp.floor(value * scale + 0.5).astype(jnp.int32)
                    send_q[g, d, kind * STRIP:(kind + 1) * STRIP, lanes] = level.astype(jnp.int16)

        for d in range(targets):
            send_r[g, d, :, width:width + LANES] = jnp.full((1, LANES), smooth_ref[0, 5])

        @pl.loop(1, targets)
        def _(hop):
            for copy in copies(g, hop):
                copy.start()

        recv_s[g, targets - 1] = send_s[g, me]
        recv_q[g, targets - 1] = send_q[g, me]
        recv_r[g, targets - 1] = send_r[g, me]

    @pl.loop(0, strips)
    def _(k):
        columns(k)

        @pl.when(jnp.logical_and(k == 0, has_low))
        def _():
            halo(0).start()

        @pl.when(jnp.logical_and(k == strips - 1, has_high))
        def _():
            halo(1).start()

        @pl.when(k >= 1)
        def _():
            records(k)

    @pl.when(has_low)
    def _():
        halo(0).wait_send()

    @pl.when(has_high)
    def _():
        halo(0).wait_recv()

    @pl.when(has_high)
    def _():
        halo(1).wait_send()

    @pl.when(has_low)
    def _():
        halo(1).wait_recv()

    records(0)

    @pl.loop(0, strips)
    def _(turn):
        g = lax.rem(turn + 1, strips)

        @pl.loop(1, targets)
        def _(hop):
            for copy in copies(g, hop):
                copy.wait()

        peak = recv_s[g, 0]
        for p in range(1, targets):
            peak = jnp.maximum(peak, recv_s[g, p])
        summed = jnp.zeros_like(peak)
        totals = [jnp.zeros_like(peak) for _ in range(3)]
        for p in range(targets):
            weight = jnp.exp(recv_s[g, p] - peak)
            summed = summed + weight
            totals[0] = totals[0] + weight * recv_r[g, p, :, width:width + 1]
            scaled = weight * recv_r[g, p, :, 0:width]
            for kind in range(2):
                level = recv_q[g, p, kind * STRIP:(kind + 1) * STRIP, :]
                totals[1 + kind] = totals[1 + kind] + scaled * level.astype(jnp.int32).astype(
                    jnp.float32)
        merged = jnp.concatenate([total / summed for total in totals], axis=0)
        placed = jnp.zeros_like(merged)
        for _ in range(3):
            term = merged.astype(jnp.bfloat16)
            placed = placed + jnp.dot(term, order_ref[...], preferred_element_type=jnp.float32)
            merged = merged - term.astype(jnp.float32)
        for n, run in enumerate(rows_of(g)):
            rows = pl.ds(run, 8)
            map_ref[rows, :] = placed[8 * n:8 * n + 8]
            field_ref[0, rows, :] = placed[STRIP + 8 * n:STRIP + 8 * n + 8]
            field_ref[1, rows, :] = placed[2 * STRIP + 8 * n:2 * STRIP + 8 * n + 8]


def refocus(smooth, rows, phase, spectra, count, targets):
    band = Y_WIN // count
    strips = band // STRIP
    groups = SLABS // targets
    width = groups * LANES
    piece = LANES // targets
    chips = count // CORES
    units = strips * NX // UNIT
    half_rows = chips * 2 * STRIP
    pair = pair_of(band)
    lane = np.arange(LANES)
    twist = np.arange(SLABS)[:, None] * lane[None, :] * (2.0 * np.pi / NX)
    twist = np.stack([np.cos(twist), np.sin(twist)]).astype(np.float32)
    angle = lane[:, None] * lane[None, :] % LANES * (2.0 * np.pi / LANES)
    cosine, sine = np.cos(angle) / NX, np.sin(angle) / NX
    dft = np.block([[cosine, sine], [-sine, cosine]]).astype(np.float32)
    spot = np.arange(width)
    slab = spot // LANES * targets + spot % LANES // piece
    order = np.zeros((width, width), np.float32)
    order[spot, spot % piece * SLABS + slab] = 1.0
    vmem = pl.BlockSpec(memory_space=pltpu.VMEM)
    codes = [
        pltpu.VMEM((units, chips - 1, 3 * STRIP, UNIT), jnp.int16),
        pltpu.VMEM((units, chips - 1, 1, UNIT), jnp.float32),
    ]
    records = [
        pltpu.VMEM((strips, targets, STRIP, width), jnp.float32),
        pltpu.VMEM((strips, targets, 2 * STRIP, width), jnp.int16),
        pltpu.VMEM((strips, targets, 1, width + LANES), jnp.float32),
    ]
    return pl.pallas_call(
        partial(kernel, count),
        out_shape=(jax.ShapeDtypeStruct((band, width), jnp.float32),
                   jax.ShapeDtypeStruct((2, band, width), jnp.float32)),
        in_specs=[pl.BlockSpec(memory_space=pltpu.SMEM)] + [vmem] * 7
        + [pl.BlockSpec(memory_space=pl.ANY)],
        out_specs=(vmem, vmem),
        scratch_shapes=[
            pltpu.VMEM((strips // pair, pair * 2 * CORES * half_rows, spectra.shape[0]),
                       jnp.bfloat16),
            pltpu.VMEM((NX // UNIT, spectra.shape[0], UNIT), jnp.bfloat16),
            pltpu.VMEM((units, CORES * half_rows, UNIT), jnp.float32),
            pltpu.VMEM((units, half_rows, UNIT), jnp.float32),
            pltpu.VMEM((units, half_rows, UNIT), jnp.float32),
            *codes, *codes,
            pltpu.VMEM((2 * STRIP, NX), jnp.float32),
            pltpu.VMEM((SLABS, STRIP, 2 * LANES), jnp.float32),
            pltpu.VMEM((2, SLABS, band, LANES), jnp.float32),
            pltpu.VMEM((SLABS + 2, band + 16, LANES), jnp.float32),
            pltpu.VMEM((SLABS + 2 * MAXWIDTH, STRIP, LANES), jnp.float32),
            pltpu.VMEM((SLABS, STRIP, LANES), jnp.float32),
            *records, *records,
            pltpu.SemaphoreType.DMA((NX // UNIT,)),
            pltpu.SemaphoreType.DMA((units,)),
            pltpu.SemaphoreType.DMA((units,)),
            pltpu.SemaphoreType.DMA((units, chips - 1, 2)),
            pltpu.SemaphoreType.DMA((units, chips - 1, 2)),
            pltpu.SemaphoreType.DMA((2,)),
            pltpu.SemaphoreType.DMA((2,)),
            pltpu.SemaphoreType.DMA((strips, targets - 1, 3)),
            pltpu.SemaphoreType.DMA((strips, targets - 1, 3)),
        ],
        compiler_params=pltpu.CompilerParams(
            collective_id=0, has_side_effects=True, vmem_limit_bytes=VMEM_BYTES),
    )(smooth, *rows, phase, jnp.asarray(twist), jnp.asarray(dft),
      jnp.asarray(order, jnp.bfloat16), spectra)


def shards(spectrum, plane_index, kernel_width, focus_gain):
    count = lax.axis_size("rows")
    targets = lax.axis_size("depth")
    place = lax.axis_index("rows")
    plane, radius = plane_index[0], kernel_width[0]
    rows = row_phases(plane, place, count)
    spectra = spectrum.reshape(2 * spectrum.shape[1], NX)
    phase = line_phase(plane, jnp.arange(NX, dtype=jnp.int32))
    phase = jnp.stack([jnp.cos(phase), jnp.sin(phase)])
    inside = (jnp.arange(1, MAXWIDTH + 1) <= radius).astype(jnp.float32)
    smooth = jnp.concatenate([
        (2 * radius + 1).astype(jnp.float32)[None], inside, focus_gain,
        plane_index.astype(jnp.float32) / DEPTHS])[None]
    return refocus(smooth, rows, phase, spectra, count, targets)


def solution(mesh):
    return jax.shard_map(
        shards,
        mesh=mesh,
        in_specs=(P(None, "rows", None), P("depth"), P("depth"), P("depth")),
        out_specs=(P("rows", "depth"), P(None, "rows", "depth")),
        check_vma=False,
    )
```

```python
from functools import partial
import math

import numpy as np
import jax
import jax.numpy as jnp
from jax import lax
from jax.experimental import pallas as pl
from jax.experimental.pallas import tpu as pltpu
from jax.sharding import PartitionSpec as P

NX = 4096
Y_WIN = 256
DEPTHS = 2048
MAXWIDTH = 3
LANES = 128
SLABS = NX // LANES
CORES = 2
UNIT = 512
STRIP = 16
STEPS = 32767.0
TINY = 1e-33
FINE_STEPS = 8388000.0
FINE_TINY = 1e-30
VMEM_BYTES = 56 * 1024 * 1024


def line_phase(plane, freqs):
    signed = jnp.where(freqs < NX // 2, freqs, freqs - NX)
    square = signed * signed
    turns = (plane * (square % NX) + NX * (plane * (square // NX) % NX)) % (NX * NX)
    return turns.astype(jnp.float32) * (-2.0 * math.pi / (NX * NX))


def pair_of(band):
    return 2 if band // STRIP % 2 == 0 else 1


def row_order(values, count):
    band = Y_WIN // count
    split = values.reshape(count // CORES, CORES, band // STRIP, STRIP, -1)
    return split.transpose(2, 1, 0, 3, 4).reshape(Y_WIN, -1)


def row_phases(plane, place, count):
    freqs_n = NX // count
    turns = np.arange(Y_WIN)[:, None] * np.arange(freqs_n)[None, :] % NX
    angle = row_order(turns * (2.0 * np.pi / NX), count)
    base = np.stack([np.cos(angle), np.sin(angle)]).astype(np.float32)
    phase = line_phase(plane, place * freqs_n + jnp.arange(freqs_n, dtype=jnp.int32))
    rows = row_order(np.arange(Y_WIN, dtype=np.int32), count)
    start = (place * freqs_n * jnp.asarray(rows) % NX).astype(jnp.float32)
    start = start * (2.0 * math.pi / NX)
    return (jnp.asarray(base), jnp.stack([jnp.cos(phase), jnp.sin(phase)]),
            jnp.stack([jnp.cos(start), jnp.sin(start)]))


def butterflies(real, imag):
    n = len(real)
    if n == 1:
        return real, imag
    even_r, even_i = butterflies(real[0::2], imag[0::2])
    odd_r, odd_i = butterflies(real[1::2], imag[1::2])
    out_r, out_i = [None] * n, [None] * n
    for k in range(n // 2):
        c, s = math.cos(2.0 * math.pi * k / n), math.sin(2.0 * math.pi * k / n)
        if k == 0:
            tr, ti = odd_r[k], odd_i[k]
        elif 4 * k == n:
            tr, ti = -odd_i[k], odd_r[k]
        else:
            tr, ti = odd_r[k] * c - odd_i[k] * s, odd_r[k] * s + odd_i[k] * c
        out_r[k], out_i[k] = even_r[k] + tr, even_i[k] + ti
        out_r[k + n // 2], out_i[k + n // 2] = even_r[k] - tr, even_i[k] - ti
    return out_r, out_i


def fine_code(value):
    largest = jnp.max(jnp.abs(value), axis=0, keepdims=True)
    largest = jnp.maximum(largest, FINE_TINY)
    level = jnp.floor(value * (FINE_STEPS / largest) + 0.5).astype(jnp.int32)
    upper = (level + 128) >> 8
    rest = level - (upper << 8)
    packed = jnp.maximum(rest[:STRIP], -127) * 256 + rest[STRIP:]
    return upper.astype(jnp.int16), packed.astype(jnp.int16), largest * (1.0 / FINE_STEPS)


def fine_value(upper, packed, unit):
    packed = packed.astype(jnp.int32)
    second = ((packed + 128) & 255) - 128
    rest = jnp.concatenate([(packed - second) >> 8, second], axis=0)
    return (upper.astype(jnp.int32) * 256 + rest).astype(jnp.float32) * unit


def wrapped(block, forward):
    lane = lax.broadcasted_iota(jnp.int32, block.shape, block.ndim - 1)
    shift = LANES - 1 if forward else 1
    edge = LANES - 1 if forward else 0
    return jnp.where(lane == edge, 0.0, pltpu.roll(block, shift, block.ndim - 1))


def kernel(count, smooth_ref, base_ref, turn_ref, start_ref, phase_ref, twist_ref, dft_ref, order_ref, spec_ref,
           map_ref, field_ref, table, spec, part, core_in, half,
           code_out, unit_out, code_in, unit_in, strip_sum, mid, pic, rim, energy, score,
           send_s, send_q, send_r, recv_s, recv_q, recv_r,
           loads, a_send, a_recv, b_send, b_recv, halo_send, halo_recv, sends, recvs):
    strips, targets, _, width = send_s.shape
    band = strips * STRIP
    groups = width // LANES
    piece = LANES // targets
    chips = count // CORES
    parts_n = NX // UNIT
    units = strips * parts_n
    half_rows = half.shape[1]
    block = 2 * STRIP
    place, me = lax.axis_index("rows"), lax.axis_index("depth")
    core, chip = lax.rem(place, CORES), lax.div(place, CORES)
    partner = chip * CORES + 1 - core
    has_low, has_high = place > 0, place < count - 1

    def load(c):
        return pltpu.make_async_copy(
            spec_ref.at[:, pl.ds(c * UNIT, UNIT)], spec.at[c], loads.at[c])

    def other(hop):
        return lax.rem(chip + hop, chips)

    def remote(src, dst, send, recv, target):
        return pltpu.make_async_remote_copy(
            src_ref=src, dst_ref=dst, send_sem=send, recv_sem=recv,
            device_id=target, device_id_type=pl.DeviceIdType.MESH)

    def core_copy(u):
        rows = pl.ds(pl.multiple_of((1 - core) * half_rows, half_rows), half_rows)
        return remote(part.at[u, rows], core_in.at[u], a_send.at[u], a_recv.at[u],
                      {"rows": partner})

    def chip_copies(u, hop):
        return [remote(src.at[u, hop - 1], dst.at[u, hop - 1], b_send.at[u, hop - 1, i],
                       b_recv.at[u, hop - 1, i], {"rows": other(hop) * CORES + core})
                for i, (src, dst) in enumerate(((code_out, code_in), (unit_out, unit_in)))]

    def halo(kind):
        low = kind == 0
        own = pl.ds(8 if low else band, 8)
        there = pl.ds(8 + band if low else 0, 8)
        return remote(rim.at[pl.ds(1, SLABS), own], rim.at[pl.ds(1, SLABS), there],
                      halo_send.at[kind], halo_recv.at[kind],
                      {"rows": lax.rem(place + (count - 1 if low else 1), count)})

    def copies(s, hop):
        target = lax.rem(me + hop, targets)
        return [remote(src.at[s, target], dst.at[s, hop - 1], sends.at[s, hop - 1, i],
                       recvs.at[s, hop - 1, i], {"depth": target})
                for i, (src, dst) in enumerate(
                    ((send_s, recv_s), (send_q, recv_q), (send_r, recv_r)))]

    for c in range(parts_n):
        load(c).start()

    barrier = pltpu.get_barrier_semaphore()

    def greet(target):
        pl.semaphore_signal(barrier, inc=1, device_id=target,
                            device_id_type=pl.DeviceIdType.MESH)

    greet({"rows": partner})
    for hop in range(1, chips):
        greet({"rows": other(hop) * CORES + core})

    @pl.when(has_low)
    def _():
        greet({"rows": place - 1})

    @pl.when(has_high)
    def _():
        greet({"rows": place + 1})

    @pl.loop(1, targets)
    def _(hop):
        greet({"depth": lax.rem(me + hop, targets)})

    pl.semaphore_wait(barrier, chips + targets - 1 + has_low.astype(jnp.int32)
                      + has_high.astype(jnp.int32))

    @pl.when(place == 0)
    def _():
        rim[1:SLABS + 1, 0:8, :] = jnp.zeros((SLABS, 8, LANES), jnp.float32)

    @pl.when(place == count - 1)
    def _():
        rim[1:SLABS + 1, 8 + band:16 + band, :] = jnp.zeros((SLABS, 8, LANES), jnp.float32)

    def pass_on(u):
        core_copy(u).wait()
        rows = pl.ds(pl.multiple_of(core * half_rows, half_rows), half_rows)
        half[u] = part[u, rows] + core_in[u]
        for hop in range(1, chips):
            rows = pl.ds(pl.multiple_of(other(hop) * block, block), block)
            upper, packed, unit = fine_code(half[u, rows])
            code_out[u, hop - 1, 0:block, :] = upper
            code_out[u, hop - 1, block:block + STRIP, :] = packed
            unit_out[u, hop - 1] = unit
            for copy in chip_copies(u, hop):
                copy.start()

    pair = pair_of(band)
    part_rows = CORES * half_rows

    def unit_of(p, c, i):
        return (p * pair + i) * parts_n + c

    def pass_all(p, c):
        for i in range(pair):
            pass_on(unit_of(p, c, i))

    def make_table(p):
        blocks = pair * CORES * chips
        freqs_n = turn_ref.shape[1]
        pc, ps = turn_ref[0:1, :], turn_ref[1:2, :]

        @pl.loop(0, blocks)
        def _(b):
            rows = pl.ds(pl.multiple_of((p * blocks + b) * STRIP, STRIP), STRIP)
            bc, bs = base_ref[0, rows, :], base_ref[1, rows, :]
            rc, rs = start_ref[0, rows, :], start_ref[1, rows, :]
            tc, ts = rc * pc - rs * ps, rc * ps + rs * pc
            real, imag = bc * tc - bs * ts, bc * ts + bs * tc
            at = pl.multiple_of(b * block, block)
            for value, places in ((real, ((0, 0), (STRIP, freqs_n))),
                                  (imag, ((STRIP, 0),)), (-imag, ((0, freqs_n),))):
                first = value.astype(jnp.bfloat16)
                second = (value - first.astype(jnp.float32)).astype(jnp.bfloat16)
                for row, lane in places:
                    lanes = slice(lane, lane + freqs_n)
                    table[p, pl.ds(at + row, STRIP), lanes] = first
                    table[p, pl.ds(at + row + blocks * block, STRIP), lanes] = second

    def rows_transform(p):
        make_table(p)

        @pl.loop(0, parts_n)
        def _(c):
            @pl.when(p == 0)
            def _():
                load(c).wait()

            both = jnp.dot(table[p], spec[c], preferred_element_type=jnp.float32)
            for i in range(pair):
                u = unit_of(p, c, i)
                low, high = i * part_rows, (pair + i) * part_rows
                part[u] = both[low:low + part_rows] + both[high:high + part_rows]
                core_copy(u).start()

            @pl.when(c >= 1)
            def _():
                pass_all(p, c - 1)

        pass_all(p, parts_n - 1)

    @pl.loop(0, strips // pair)
    def _(p):
        rows_transform(p)

    def columns(k):
        rows = pl.ds(pl.multiple_of(chip * block, block), block)
        for c in range(parts_n):
            u = k * parts_n + c
            total = half[u, rows]
            for hop in range(1, chips):
                for copy in chip_copies(u, hop):
                    copy.wait()
                total = total + fine_value(
                    code_in[u, hop - 1, 0:block, :], code_in[u, hop - 1, block:block + STRIP, :],
                    unit_in[u, hop - 1])
            strip_sum[:, c * UNIT:(c + 1) * UNIT] = total

        @pl.loop(0, STRIP // 8)
        def _(s):
            at = pl.multiple_of(s * 8, 8)
            real, imag = [], []
            for slab in range(SLABS):
                lanes = slice(slab * LANES, (slab + 1) * LANES)
                xr = strip_sum[pl.ds(at, 8), lanes]
                xi = strip_sum[pl.ds(STRIP + at, 8), lanes]
                pc, ps = phase_ref[0:1, lanes], phase_ref[1:2, lanes]
                real.append(xr * pc - xi * ps)
                imag.append(xr * ps + xi * pc)
            real, imag = butterflies(real, imag)
            for slab in range(SLABS):
                tc, ts = twist_ref[0, slab:slab + 1, :], twist_ref[1, slab:slab + 1, :]
                mid[slab, pl.ds(at, 8), 0:LANES] = real[slab] * tc - imag[slab] * ts
                mid[slab, pl.ds(at, 8), LANES:2 * LANES] = real[slab] * ts + imag[slab] * tc

        per = 16
        at = pl.multiple_of(k * STRIP, STRIP)

        @pl.loop(0, SLABS // per)
        def _(q):
            slabs = pl.ds(q * per, per)
            rows = mid[slabs].reshape(per * STRIP, 2 * LANES)
            both = jnp.dot(rows, dft_ref[...], precision=lax.Precision.HIGHEST,
                           preferred_element_type=jnp.float32)
            real, imag = both[:, :LANES], both[:, LANES:]
            pic[0, slabs, pl.ds(at, STRIP)] = real.reshape(per, STRIP, LANES)
            pic[1, slabs, pl.ds(at, STRIP)] = imag.reshape(per, STRIP, LANES)
            rim[pl.ds(q * per + 1, per), pl.ds(at + 8, STRIP)] = (
                real * real + imag * imag).reshape(per, STRIP, LANES)

    def rows_of(g):
        return [pl.multiple_of(lax.rem(g * STRIP + band - 8, band), 8),
                pl.multiple_of(g * STRIP, 8)]

    def records(g):
        runs = rows_of(g)
        for n, run in enumerate(runs):
            window = pl.ds(run, 24)
            out = slice(8 * n, 8 * n + 8)
            rim[0, window, :] = wrapped(rim[SLABS, window, :], False)
            rim[SLABS + 1, window, :] = wrapped(rim[1, window, :], True)

            @pl.loop(0, SLABS)
            def _(slab):
                before, here, after = (rim[slab + j, window, :] for j in range(3))

                def vertical(x):
                    return x[7:15] + 2.0 * x[8:16] + x[9:17]

                across = vertical(after) - vertical(before)
                horizontal = before + 2.0 * here + after
                downward = horizontal[9:17] - horizontal[7:15]
                energy[slab + MAXWIDTH, out, :] = across * across + downward * downward

        for k in range(MAXWIDTH):
            energy[k] = wrapped(energy[SLABS + k], False)
            energy[SLABS + MAXWIDTH + k] = wrapped(energy[MAXWIDTH + k], True)

        @pl.loop(0, SLABS)
        def _(slab):
            total = energy[slab + MAXWIDTH]
            for k in range(1, MAXWIDTH + 1):
                total = total + smooth_ref[0, k] * (
                    energy[slab + MAXWIDTH - k] + energy[slab + MAXWIDTH + k])
            score[slab] = smooth_ref[0, 4] * jnp.log(1.0 + total / smooth_ref[0, 0])

        block_of = lax.broadcasted_iota(jnp.int32, (STRIP, LANES), 1) // piece

        def exchanged(held):
            gap = 1
            while gap < targets:
                low_lane = block_of // gap % 2 == 0
                for i in range(targets):
                    if i // gap % 2 == 0:
                        a, c = held[i], held[i + gap]
                        held[i] = jnp.where(low_lane, a, pltpu.roll(c, gap * piece, 1))
                        held[i + gap] = jnp.where(
                            low_lane, pltpu.roll(a, LANES - gap * piece, 1), c)
                gap *= 2
            return held

        @pl.loop(0, groups)
        def _(q):
            lanes = pl.ds(pl.multiple_of(q * LANES, LANES), LANES)
            held = exchanged([score[q * targets + i] for i in range(targets)])
            for d in range(targets):
                send_s[g, d, :, lanes] = held[d]
            real, imag = (
                exchanged([
                    jnp.concatenate([pic[kind, q * targets + i, pl.ds(run, 8), :]
                                     for run in runs], axis=0)
                    for i in range(targets)])
                for kind in range(2))
            for d in range(targets):
                largest = jnp.max(jnp.maximum(jnp.abs(real[d]), jnp.abs(imag[d])),
                                  axis=0, keepdims=True)
                largest = jnp.maximum(largest, TINY)
                send_r[g, d, :, lanes] = largest * (1.0 / STEPS)
                scale = STEPS / largest
                for kind, value in ((0, real[d]), (1, imag[d])):
                    level = jnp.floor(value * scale + 0.5).astype(jnp.int32)
                    send_q[g, d, kind * STRIP:(kind + 1) * STRIP, lanes] = level.astype(jnp.int16)

        for d in range(targets):
            send_r[g, d, :, width:width + LANES] = jnp.full((1, LANES), smooth_ref[0, 5])

        @pl.loop(1, targets)
        def _(hop):
            for copy in copies(g, hop):
                copy.start()

        recv_s[g, targets - 1] = send_s[g, me]
        recv_q[g, targets - 1] = send_q[g, me]
        recv_r[g, targets - 1] = send_r[g, me]

    @pl.loop(0, strips)
    def _(k):
        columns(k)

        @pl.when(jnp.logical_and(k == 0, has_low))
        def _():
            halo(0).start()

        @pl.when(jnp.logical_and(k == strips - 1, has_high))
        def _():
            halo(1).start()

        @pl.when(k >= 1)
        def _():
            records(k)

    @pl.when(has_low)
    def _():
        halo(0).wait_send()

    @pl.when(has_high)
    def _():
        halo(0).wait_recv()

    @pl.when(has_high)
    def _():
        halo(1).wait_send()

    @pl.when(has_low)
    def _():
        halo(1).wait_recv()

    records(0)

    @pl.loop(0, strips)
    def _(turn):
        g = lax.rem(turn + 1, strips)

        @pl.loop(1, targets)
        def _(hop):
            for copy in copies(g, hop):
                copy.wait()

        peak = recv_s[g, 0]
        for p in range(1, targets):
            peak = jnp.maximum(peak, recv_s[g, p])
        summed = jnp.zeros_like(peak)
        totals = [jnp.zeros_like(peak) for _ in range(3)]
        for p in range(targets):
            weight = jnp.exp(recv_s[g, p] - peak)
            summed = summed + weight
            totals[0] = totals[0] + weight * recv_r[g, p, :, width:width + 1]
            scaled = weight * recv_r[g, p, :, 0:width]
            for kind in range(2):
                level = recv_q[g, p, kind * STRIP:(kind + 1) * STRIP, :]
                totals[1 + kind] = totals[1 + kind] + scaled * level.astype(jnp.int32).astype(
                    jnp.float32)
        merged = jnp.concatenate([total / summed for total in totals], axis=0)
        placed = jnp.zeros_like(merged)
        for _ in range(3):
            term = merged.astype(jnp.bfloat16)
            placed = placed + jnp.dot(term, order_ref[...], preferred_element_type=jnp.float32)
            merged = merged - term.astype(jnp.float32)
        for n, run in enumerate(rows_of(g)):
            rows = pl.ds(run, 8)
            map_ref[rows, :] = placed[8 * n:8 * n + 8]
            field_ref[0, rows, :] = placed[STRIP + 8 * n:STRIP + 8 * n + 8]
            field_ref[1, rows, :] = placed[2 * STRIP + 8 * n:2 * STRIP + 8 * n + 8]


def refocus(smooth, rows, phase, spectra, count, targets):
    band = Y_WIN // count
    strips = band // STRIP
    groups = SLABS // targets
    width = groups * LANES
    piece = LANES // targets
    chips = count // CORES
    units = strips * NX // UNIT
    half_rows = chips * 2 * STRIP
    pair = pair_of(band)
    lane = np.arange(LANES)
    twist = np.arange(SLABS)[:, None] * lane[None, :] * (2.0 * np.pi / NX)
    twist = np.stack([np.cos(twist), np.sin(twist)]).astype(np.float32)
    angle = lane[:, None] * lane[None, :] % LANES * (2.0 * np.pi / LANES)
    cosine, sine = np.cos(angle) / NX, np.sin(angle) / NX
    dft = np.block([[cosine, sine], [-sine, cosine]]).astype(np.float32)
    spot = np.arange(width)
    slab = spot // LANES * targets + spot % LANES // piece
    order = np.zeros((width, width), np.float32)
    order[spot, spot % piece * SLABS + slab] = 1.0
    vmem = pl.BlockSpec(memory_space=pltpu.VMEM)
    codes = [
        pltpu.VMEM((units, chips - 1, 3 * STRIP, UNIT), jnp.int16),
        pltpu.VMEM((units, chips - 1, 1, UNIT), jnp.float32),
    ]
    records = [
        pltpu.VMEM((strips, targets, STRIP, width), jnp.float32),
        pltpu.VMEM((strips, targets, 2 * STRIP, width), jnp.int16),
        pltpu.VMEM((strips, targets, 1, width + LANES), jnp.float32),
    ]
    return pl.pallas_call(
        partial(kernel, count),
        out_shape=(jax.ShapeDtypeStruct((band, width), jnp.float32),
                   jax.ShapeDtypeStruct((2, band, width), jnp.float32)),
        in_specs=[pl.BlockSpec(memory_space=pltpu.SMEM)] + [vmem] * 7
        + [pl.BlockSpec(memory_space=pl.ANY)],
        out_specs=(vmem, vmem),
        scratch_shapes=[
            pltpu.VMEM((strips // pair, pair * 2 * CORES * half_rows, spectra.shape[0]),
                       jnp.bfloat16),
            pltpu.VMEM((NX // UNIT, spectra.shape[0], UNIT), jnp.bfloat16),
            pltpu.VMEM((units, CORES * half_rows, UNIT), jnp.float32),
            pltpu.VMEM((units, half_rows, UNIT), jnp.float32),
            pltpu.VMEM((units, half_rows, UNIT), jnp.float32),
            *codes, *codes,
            pltpu.VMEM((2 * STRIP, NX), jnp.float32),
            pltpu.VMEM((SLABS, STRIP, 2 * LANES), jnp.float32),
            pltpu.VMEM((2, SLABS, band, LANES), jnp.float32),
            pltpu.VMEM((SLABS + 2, band + 16, LANES), jnp.float32),
            pltpu.VMEM((SLABS + 2 * MAXWIDTH, STRIP, LANES), jnp.float32),
            pltpu.VMEM((SLABS, STRIP, LANES), jnp.float32),
            *records, *records,
            pltpu.SemaphoreType.DMA((NX // UNIT,)),
            pltpu.SemaphoreType.DMA((units,)),
            pltpu.SemaphoreType.DMA((units,)),
            pltpu.SemaphoreType.DMA((units, chips - 1, 2)),
            pltpu.SemaphoreType.DMA((units, chips - 1, 2)),
            pltpu.SemaphoreType.DMA((2,)),
            pltpu.SemaphoreType.DMA((2,)),
            pltpu.SemaphoreType.DMA((strips, targets - 1, 3)),
            pltpu.SemaphoreType.DMA((strips, targets - 1, 3)),
        ],
        compiler_params=pltpu.CompilerParams(
            collective_id=0, has_side_effects=True, vmem_limit_bytes=VMEM_BYTES),
    )(smooth, *rows, phase, jnp.asarray(twist), jnp.asarray(dft),
      jnp.asarray(order, jnp.bfloat16), spectra)


def shards(spectrum, plane_index, kernel_width, focus_gain):
    count = lax.axis_size("rows")
    targets = lax.axis_size("depth")
    place = lax.axis_index("rows")
    plane, radius = plane_index[0], kernel_width[0]
    rows = row_phases(plane, place, count)
    spectra = spectrum.reshape(2 * spectrum.shape[1], NX)
    phase = line_phase(plane, jnp.arange(NX, dtype=jnp.int32))
    phase = jnp.stack([jnp.cos(phase), jnp.sin(phase)])
    inside = (jnp.arange(1, MAXWIDTH + 1) <= radius).astype(jnp.float32)
    smooth = jnp.concatenate([
        (2 * radius + 1).astype(jnp.float32)[None], inside, focus_gain,
        plane_index.astype(jnp.float32) / DEPTHS])[None]
    return refocus(smooth, rows, phase, spectra, count, targets)


def solution(mesh):
    return jax.shard_map(
        shards,
        mesh=mesh,
        in_specs=(P(None, "rows", None), P("depth"), P("depth"), P("depth")),
        out_specs=(P("rows", "depth"), P(None, "rows", "depth")),
        check_vma=False,
    )
```
